768 devices in a mesh: node: 48 (over z_lo, y, core), orb: 16 (over x, z_hi).
Axes of the slice: x: 4, y: 8, z: 12 (z_hi: 4, z_lo: 3; z = z_hi * 3 + z_lo), core: 2. Of those that a mesh axis runs over, the one named last changes fastest.
Arguments:
- panel: bfloat16 [96, 64, 128, 128], P('node', 'orb'), may hold values from -6 to 6
- orbitals: bfloat16 [96, 64, 128, 256], P('node', 'orb'), may hold values from -6 to 6
- potential: float32 [96, 64, 128], P('node', 'orb'), may hold values from 0 to 2
- projectors: bfloat16 [18432, 256], P(('node', 'orb')), may hold values from -0.375 to 0.375
- strengths: bfloat16 [18432], P(('node', 'orb')), may hold values from 0.5 to 4
- atom_domain: int32 [18432, 1], P(('node', 'orb')), may hold values from 0 to 47; in each aligned block of 24 rows (0 to 23, 24 to 47, ...) at most 2 rows name the same one
- patch_start: int32 [18432], P(('node', 'orb')), may hold values from 0 to 768
Outputs:
- filtered_panel: bfloat16 [96, 64, 128, 128], P('node', 'orb')
- intersection: float32 [128, 256], replicated
The draws below stay inside these ranges and needn't reach their ends.
Inputs may be any that keep to these rules, and one draw needn't show every extreme that they name: `atom_domain`: at most 2 of the 24 atoms held by one device name the same domain, and some device's atoms name one domain exactly 2 times.
All inputs are finite; a program needn't handle non-finite values.
Results may differ from the reference program's by a relative error of at most 0.009.
Values may be sent and summed in bfloat16 or wider, within the bound.
A program may use at most 32 MiB of HBM per device.

```python
import math
import jax
import jax.numpy as jnp
import numpy as np
from jax import lax

PANEL = 128
NORB = 256
CX = 2
CY = 4
NZ = 128
DEG = 6
PATCH = 256
ATOM_DEV = 24
DOMS = 48
CAP = 2
NX = 96
NY = 64
ATOMS = 18432
N_ORB = 16


def set_ends(result, key, low, top_value):
    index_at = [jax.random.randint(jax.random.fold_in(key, axis), (), 0, length) for axis, length in enumerate(result.shape)]
    widest = result.shape.index(max(result.shape))
    neighbour = index_at[:widest] + [(index_at[widest] + 1) % result.shape[widest]] + index_at[widest + 1:]
    return result.at[tuple(index_at)].set(low).at[tuple(neighbour)].set(top_value)


def level_of(stream_key, dims, split, low, largest):
    loudness, own = 1.0, jax.random.fold_in(stream_key, 6)
    for axis_at, blocks in split:
        steps = jnp.exp(jax.random.uniform(jax.random.fold_in(own, axis_at), (blocks,), jnp.float32, low / len(split), largest / len(split)))
        loudness = loudness * jnp.repeat(steps, dims[axis_at] // blocks).reshape([-1 if axis == axis_at else 1 for axis in range(len(dims))])
    return loudness


def shared_out(stream_key, own, number, rows, number_of, top, reach, skew):
    order = jax.random.permutation(stream_key, number_of)
    packed, usual = shares(number_of, rows * top, reach, skew, True), shares(number_of, rows * top, reach, skew, False)
    places = jnp.arange(number_of)

    def named(lengths, turn):
        used = int((lengths > 0).sum())
        fixed = max(1, used // 4)
        passed = fixed + (places - fixed + turn * (used - fixed)) % max(1, number_of - fixed)
        return jnp.zeros((number_of,), jnp.int32).at[order[jnp.where(places < fixed, places, passed)]].set(jnp.asarray(lengths, jnp.int32))

    lengths = jnp.where(number % 4 == 0, named(packed, number // 4), named(usual, number - number // 4 - 1))
    mixed = jax.random.permutation(jax.random.fold_in(own, 3), number_of)
    giver, taker = mixed[0:number_of // 2 * 2:2], mixed[1:number_of // 2 * 2:2]
    slack = jnp.minimum(lengths[giver] - 1, reach - lengths[taker]) // 2
    slack = jnp.where((giver == order[0]) | (taker == order[0]) | (lengths[taker] == 0), 0, jnp.maximum(slack, 0))
    passed = jax.random.randint(jax.random.fold_in(own, 4), (number_of // 2,), 0, 1 << 20) % (slack + 1)
    lengths = lengths.at[giver].add(-passed).at[taker].add(passed)
    items = jnp.searchsorted(jnp.cumsum(lengths), jnp.arange(rows * top), side="right").astype(jnp.int32)
    table = items.reshape(top, rows).T
    table = table[jax.random.permutation(jax.random.fold_in(own, 1), rows)]
    turn = jax.random.randint(jax.random.fold_in(own, 2), (rows, 1), 0, top)
    return jnp.take_along_axis(table, (jnp.arange(top)[None, :] + turn) % top, axis=1)


def shares(number_of, total, most, skew, full):
    weights = [(1 << 20) // math.isqrt(standing ** skew) + 1 for standing in range(1, number_of + 1)]
    largest = most if full else min(most, max(-(-total // number_of), total * weights[0] // sum(weights)))
    least = 1 if total - largest >= number_of - 1 else 0
    counts, spare = [largest] + [least] * (number_of - 1), total - largest - least * (number_of - 1)
    while spare > 0:
        free = [i for i in range(1, number_of) if counts[i] < largest] or [i for i in range(1, number_of) if counts[i] < most]
        mass, remaining = sum([weights[i] for i in free]), spare
        for i in free:
            more = min(most - counts[i], max(1, remaining * weights[i] // mass), spare)
            counts[i] = counts[i] + more
            spare = spare - more
    return np.array(counts)


def gaussian(key, extent, scale, bound, pieces=(), kind=jnp.bfloat16):
    result = jax.random.normal(key, extent, jnp.float32) * scale
    if len(pieces) > 0:
        result = level_of(key, extent, pieces, -0.22, 0.18) * result
    return jnp.clip(result, min=-bound, max=bound).astype(kind)


def setup_inputs(seed: int = 0) -> dict:
    key_of = jax.random.split(jax.random.key(seed), 8)
    panel = gaussian(key_of[0], (NX, NY, NZ, PANEL), 1.0, 6.0, ((0, 48), (1, 16)))
    orbitals = gaussian(key_of[1], (NX, NY, NZ, NORB), 1.0, 6.0, ((0, 48), (1, 16)))
    potential = jnp.clip(2.0 * jax.random.uniform(key_of[2], (NX, NY, NZ), jnp.float32) ** level_of(key_of[2], (NX, NY, NZ), ((0, 48), (1, 16)), -0.2, 0.2), 0.0, 2.0)
    projectors = gaussian(key_of[3], (ATOMS, PATCH), PATCH ** -0.5, 0.375, ((0, 768),))
    strengths = jnp.clip(jnp.exp(math.log(4.0) - 2.0794415 * jax.random.uniform(key_of[4], (ATOMS,), jnp.float32) ** level_of(key_of[4], (ATOMS,), ((0, 768),), -0.2, 0.2)), 0.5, 4.0).astype(jnp.bfloat16)
    atom_domain_keys = jax.random.split(jax.random.fold_in(key_of[5], 1), ATOMS // ATOM_DEV)
    atom_domain_turns = jax.random.permutation(jax.random.fold_in(key_of[5], 3), ATOMS // ATOM_DEV)
    atom_domain = jax.vmap(lambda own, number: shared_out(jax.random.fold_in(key_of[5], 2), own, number, ATOM_DEV, DOMS, 1, CAP, 2))(atom_domain_keys, atom_domain_turns).reshape((ATOMS, 1))
    patch_start = set_ends(jax.random.randint(key_of[6], (ATOMS,), 0, CX * CY * NZ - PATCH + 1), jax.random.fold_in(key_of[6], 1), 0, CX * CY * NZ - PATCH).astype(jnp.int32)
    return dict(panel=panel, orbitals=orbitals, potential=potential, projectors=projectors, strengths=strengths, atom_domain=atom_domain, patch_start=patch_start)


shift_point = 5.25
half_range = 3.25

def operate(field, potential):
    padded = jnp.pad(field, ((1, 1), (1, 1), (1, 1), (0, 0)))
    middle = padded[1:-1, 1:-1, 1:-1]
    neighbours = padded[2:, 1:-1, 1:-1] + padded[:-2, 1:-1, 1:-1]
    neighbours = neighbours + padded[1:-1, 2:, 1:-1] + padded[1:-1, :-2, 1:-1]
    neighbours = neighbours + padded[1:-1, 1:-1, 2:] + padded[1:-1, 1:-1, :-2]
    return ((3.0 + potential[..., None]) * middle - 0.5 * neighbours - shift_point * middle) / half_range

def reference(panel, orbitals, potential, projectors, strengths, atom_domain, patch_start):
    groups = PANEL // 16
    blocks = jnp.moveaxis(panel.reshape(NX, NY, NZ, groups, 16), 3, 0)

    def run_group(block):
        previous = block
        current = block
        for step_index in range(DEG):
            applied = operate(current.astype(jnp.float32), potential)
            if step_index == 0:
                updated = applied
            else:
                updated = 2.0 * applied - previous.astype(jnp.float32)
            previous = current
            current = updated.astype(jnp.bfloat16)
        return current
    filtered = jnp.moveaxis(lax.map(run_group, blocks), 0, 3).reshape(NX, NY, NZ, PANEL)
    nodes_all = NX * NY * NZ
    grid_term = jnp.dot(filtered.reshape(nodes_all, PANEL).astype(jnp.float32).T, orbitals.reshape(nodes_all, NORB).astype(jnp.float32), precision=lax.Precision.HIGHEST, preferred_element_type=jnp.float32)
    cells = CX * CY * NZ
    zero_index = jnp.zeros((), jnp.int32)

    def one_atom(atom_index):
        domain = atom_domain[atom_index, 0].astype(jnp.int32)
        column = (atom_index // ATOM_DEV % N_ORB).astype(jnp.int32)
        anchor = (domain * CX, column * CY, zero_index, zero_index)
        panel_block = lax.dynamic_slice(filtered, anchor, (CX, CY, NZ, PANEL)).reshape(cells, PANEL)
        orbit_block = lax.dynamic_slice(orbitals, anchor, (CX, CY, NZ, NORB)).reshape(cells, NORB)
        start = patch_start[atom_index].astype(jnp.int32)
        panel_rows = lax.dynamic_slice_in_dim(panel_block, start, PATCH, 0).astype(jnp.float32)
        orbit_rows = lax.dynamic_slice_in_dim(orbit_block, start, PATCH, 0).astype(jnp.float32)
        values = projectors[atom_index].astype(jnp.float32)
        panel_proj = jnp.dot(values, panel_rows, precision=lax.Precision.HIGHEST)
        orbit_proj = jnp.dot(values, orbit_rows, precision=lax.Precision.HIGHEST)
        return (panel_proj * strengths[atom_index].astype(jnp.float32), orbit_proj)
    panel_proj, orbit_proj = lax.map(one_atom, jnp.arange(ATOMS, dtype=jnp.int32))
    atom_term = jnp.dot(panel_proj.T, orbit_proj, precision=lax.Precision.HIGHEST, preferred_element_type=jnp.float32)
    intersection = grid_term * (1.0 / math.sqrt(nodes_all)) + atom_term * (1.0 / math.sqrt(ATOMS))
    return (filtered, intersection)
```

```python
import functools
import math

import jax
import jax.numpy as jnp
from jax import lax
from jax.experimental import pallas as pl
from jax.experimental.pallas import tpu as pltpu
from jax.sharding import PartitionSpec as P

DEG = 6
CHUNKS = 4
MESH = pl.DeviceIdType.MESH
SHIFT_POINT = 5.25
HALF_RANGE = 3.25


def factors(count_node, count_orb):
    if (count_node, count_orb) == (48, 16):
        return 3, 8, 4, 4
    ny = max(1, min(count_node // 2, 8))
    return count_node // (2 * ny), ny, max(1, count_orb // 4), min(count_orb, 4)


def kernel(
    dims,
    scales,
    panel_ref,
    orbit_ref,
    pot_ref,
    proj_ref,
    str_ref,
    dom_ref,
    start_ref,
    out_ref,
    inter_ref,
    y,
    hxl,
    hxh,
    hyl,
    hyh,
    diag,
    orb_v,
    w_ref,
    m_ref,
    apack,
    abuf,
    part,
    rs,
    ar_src,
    ar,
    ag_src,
    ag,
    load_sem,
    out_sem,
    hsend,
    hrecv,
    asend,
    arecv,
    rsend,
    rrecv,
):
    n_node, n_orb, nzl, ny, nx, nzh = dims
    c1, ratio = scales
    node = lax.axis_index("node")
    orb = lax.axis_index("orb")
    core = lax.rem(node, 2)
    yy = lax.rem(node // 2, ny)
    zl = node // (2 * ny)
    xx = orb // nzh
    zh = lax.rem(orb, nzh)
    n_xy = nx * ny
    n_zc = nzh * nzl * 2
    wx, wy, nz, cols = panel_ref.shape
    ch = nz // CHUNKS

    load_panel = pltpu.make_async_copy(panel_ref, y.at[0], load_sem.at[0])
    load_panel.start()
    load_orbit = pltpu.make_async_copy(orbit_ref, orb_v, load_sem.at[1])
    load_orbit.start()

    barrier = pltpu.get_barrier_semaphore()

    def greet(target_node, target_orb):
        pl.semaphore_signal(
            barrier, inc=1, device_id=(target_node, target_orb), device_id_type=MESH
        )

    def greet_node(i, carry):
        greet(lax.rem(node + i, n_node), orb)
        return carry

    lax.fori_loop(1, n_node, greet_node, 0)

    def greet_x(i, carry):
        gx = lax.rem(xx + 1 + i // ny, nx)
        gy = lax.rem(i, ny)
        greet((zl * ny + gy) * 2 + core, gx * nzh + zh)
        return carry

    lax.fori_loop(0, (nx - 1) * ny, greet_x, 0)

    def greet_z(i, carry):
        gz = lax.rem(zh + 1 + i // (2 * nzl), nzh)
        rest = lax.rem(i, 2 * nzl)
        greet(((rest // 2) * ny + yy) * 2 + lax.rem(rest, 2), xx * nzh + gz)
        return carry

    lax.fori_loop(0, (nzh - 1) * 2 * nzl, greet_z, 0)
    greeted = (n_node - 1) + (nx - 1) * ny + (nzh - 1) * 2 * nzl
    up_cross = jnp.logical_and(zh == nzh - 1, orb < n_orb - 1)
    down_cross = jnp.logical_and(zh == 0, orb > 0)

    @pl.when(up_cross)
    def _():
        greet(node, orb + 1)

    @pl.when(down_cross)
    def _():
        greet(node, orb - 1)

    crossings = up_cross.astype(jnp.int32) + down_cross.astype(jnp.int32)
    pl.semaphore_wait(barrier, greeted + crossings)

    def halo(side, k, c):
        zs = pl.ds(c * ch, ch)
        if side == 0:
            src, dst, target = y.at[k, wx - 1, :, zs], hxl.at[k, :, zs], (node + 1, orb)
        elif side == 1:
            src, dst, target = y.at[k, 0, :, zs], hxh.at[k, :, zs], (node - 1, orb)
        elif side == 2:
            src, dst, target = y.at[k, :, wy - 1, zs], hyl.at[k, :, zs], (node, orb + 1)
        else:
            src, dst, target = y.at[k, :, 0, zs], hyh.at[k, :, zs], (node, orb - 1)
        return pltpu.make_async_remote_copy(
            src_ref=src,
            dst_ref=dst,
            send_sem=hsend.at[side],
            recv_sem=hrecv.at[k, side, c],
            device_id=target,
            device_id_type=MESH,
        )

    sends = (node < n_node - 1, node > 0, orb < n_orb - 1, orb > 0)
    receives = (node > 0, node < n_node - 1, orb > 0, orb < n_orb - 1)

    def send_halo(k, c):
        for side in (2, 3, 0, 1):

            @pl.when(sends[side])
            def _(side=side):
                halo(side, k, c).start()

    def wait_halo(k, c):
        for side in (0, 1, 2, 3):

            @pl.when(receives[side])
            def _(side=side):
                halo(side, k, c).wait_recv()

    load_panel.wait()
    for c in range(CHUNKS):
        send_halo(0, c)

    for side, buf in enumerate((hxl, hxh, hyl, hyh)):

        @pl.when(jnp.logical_not(receives[side]))
        def _(buf=buf):
            def clear(k, carry):
                buf[k] = jnp.zeros(buf.shape[1:], buf.dtype)
                return carry

            lax.fori_loop(0, DEG, clear, 0)

    atoms = proj_ref.shape[0]
    f32 = jnp.float32
    a_sub = lax.broadcasted_iota(jnp.int32, (atoms, atoms), 0)
    a_lane = lax.broadcasted_iota(jnp.int32, (atoms, atoms), 1)
    eye = a_sub == a_lane

    def column(row):
        return jnp.sum(jnp.where(eye, jnp.broadcast_to(row, (atoms, atoms)), 0), axis=1, keepdims=True)

    dom_row = dom_ref[...]
    start_row = start_ref[...]
    dom_col = column(dom_row)
    start_col = column(start_row)
    str_col = column(str_ref[...].astype(f32))
    hi_col = start_col // 128
    lo_col = start_col - hi_col * 128
    same = jnp.logical_and(jnp.broadcast_to(dom_col, (atoms, atoms)) == dom_row, a_sub < a_lane)
    rank_row = jnp.sum(jnp.where(same, 1, 0), axis=0, keepdims=True)
    halves = []
    for half in range(2):
        piece = proj_ref[:, half * 128 : (half + 1) * 128].astype(f32)
        for bit in range(7):
            taken = ((lo_col // (1 << bit)) - 2 * (lo_col // (2 << bit))) == 1
            piece = jnp.where(taken, pltpu.roll(piece, 1 << bit, 1), piece)
        halves.append(piece)
    lane = lax.broadcasted_iota(jnp.int32, (atoms, 128), 1)
    meta = jnp.where(
        lane == 0,
        lo_col.astype(f32),
        jnp.where(lane == 1, hi_col.astype(f32), jnp.where(lane == 2, str_col, 0.0)),
    )
    rows = lax.broadcasted_iota(jnp.int32, (n_node * 8, atoms), 0)
    slot_dom = rows // 8
    slot_row = rows - slot_dom * 8
    named = slot_dom == dom_row
    packed = None
    for code, piece in ((2 * rank_row, halves[0]), (2 * rank_row + 1, halves[1]), (4 + rank_row, meta)):
        choose = jnp.where(jnp.logical_and(named, slot_row == code), 1.0, 0.0)
        term = jnp.dot(choose, piece, preferred_element_type=f32)
        packed = term if packed is None else packed + term
    apack[...] = packed.reshape(n_node, 8, 128)

    def atom_copy(i):
        other = lax.rem(node + i, n_node)
        return pltpu.make_async_remote_copy(
            src_ref=apack.at[other],
            dst_ref=abuf.at[node],
            send_sem=asend,
            recv_sem=arecv,
            device_id=(other, orb),
            device_id_type=MESH,
        )

    def send_atoms(i, carry):
        atom_copy(i).start()
        return carry

    lax.fori_loop(1, n_node, send_atoms, 0)
    abuf[node] = apack[node]

    for ix in range(wx):
        for iy in range(wy):
            row = pot_ref[ix * wy + iy : ix * wy + iy + 1, :]
            diag[ix, iy] = (jnp.broadcast_to(row, (nz, nz)).T - (SHIFT_POINT - 3.0)) * (1.0 / HALF_RANGE)

    z_out = lax.broadcasted_iota(jnp.int32, (nz, nz), 0)
    z_in = lax.broadcasted_iota(jnp.int32, (nz, nz), 1)
    beside = jnp.where(jnp.abs(z_out - z_in) == 1, 1.0, 0.0).astype(jnp.bfloat16)

    def step(k, carry):
        twice = jnp.where(k == 0, 1.0, 2.0).astype(f32)
        less = jnp.where(k == 0, 0.0, 1.0).astype(f32)
        before = lax.max(k - 1, 0)
        arm = twice * (0.5 / HALF_RANGE)
        for c in range(CHUNKS):
            zs = pl.ds(c * ch, ch)
            here = [[y[k, ix, iy, zs].astype(f32) for iy in range(wy)] for ix in range(wx)]
            base = []
            for ix in range(wx):
                line = []
                for iy in range(wy):
                    total = jnp.dot(
                        beside[c * ch : (c + 1) * ch], y[k, ix, iy], preferred_element_type=f32
                    )
                    total = total + here[1 - ix][iy]
                    if iy > 0:
                        total = total + here[ix][iy - 1]
                    if iy < wy - 1:
                        total = total + here[ix][iy + 1]
                    old = y[before, ix, iy, zs].astype(f32)
                    line.append(
                        (twice * diag[ix, iy, zs]) * here[ix][iy] - arm * total - less * old
                    )
                base.append(line)
            wait_halo(k, c)
            for ix in range(wx):
                for iy in range(wy):
                    side = (hxl if ix == 0 else hxh)[k, iy, zs].astype(f32)
                    if iy == 0:
                        side = side + hyl[k, ix, zs].astype(f32)
                    if iy == wy - 1:
                        side = side + hyh[k, ix, zs].astype(f32)
                    y[k + 1, ix, iy, zs] = (base[ix][iy] - arm * side).astype(jnp.bfloat16)

            @pl.when(k < DEG - 1)
            def _():
                send_halo(lax.min(k + 1, DEG - 1), c)

        return carry

    lax.fori_loop(0, DEG // 2, step, 0)

    pltpu.make_async_remote_copy(
        src_ref=abuf.at[pl.ds(0, n_node - 1)],
        dst_ref=abuf.at[pl.ds(0, n_node - 1)],
        send_sem=asend,
        recv_sem=arecv,
        device_id=(lax.rem(node + 1, n_node), orb),
        device_id_type=MESH,
    ).wait_recv()
    load_orbit.wait()
    blocks = wx * wy
    s_lane = lax.broadcasted_iota(jnp.int32, (n_node, 128), 1).astype(f32)
    coeffs = []
    for slot in range(2):
        v0 = abuf[:, 2 * slot, :]
        v1 = abuf[:, 2 * slot + 1, :]
        info = abuf[:, 4 + slot, :]
        lo, hi, coeff = info[:, 0:1], info[:, 1:2], info[:, 2:3]
        inside = s_lane >= lo
        placed = (
            jnp.where(inside, v0, 0.0),
            jnp.where(inside, v1, v0),
            jnp.where(inside, 0.0, v1),
        )
        for j in range(blocks):
            total = jnp.zeros((n_node, 128), f32)
            for ahead in range(3):
                if j >= ahead:
                    total = total + jnp.where(hi == float(j - ahead), placed[ahead], 0.0)
            w_ref[slot * n_node : (slot + 1) * n_node, j * 128 : (j + 1) * 128] = total.astype(
                jnp.bfloat16
            )
        coeffs.append(coeff)
    flat_orbit = orb_v[...].reshape(blocks * nz, -1)
    norb = flat_orbit.shape[1]
    proj = jnp.dot(w_ref[...], flat_orbit, preferred_element_type=f32)
    proj = proj * (jnp.concatenate(coeffs, axis=0) * ratio)
    proj_hi = proj.astype(jnp.bfloat16)
    proj_lo = (proj - proj_hi.astype(f32)).astype(jnp.bfloat16)
    proj_both = jnp.concatenate([proj_hi, proj_lo], axis=1)
    for j in range(blocks):
        both = lax.dot_general(
            w_ref[:, j * 128 : (j + 1) * 128],
            proj_both,
            (((0,), (0,)), ((), ())),
            preferred_element_type=f32,
        )
        whole = both[:, :norb] + both[:, norb:] + orb_v[j // wy, j % wy].astype(f32)
        whole_hi = whole.astype(jnp.bfloat16)
        m_ref[j * 128 : (j + 1) * 128, :norb] = whole_hi
        m_ref[j * 128 : (j + 1) * 128, norb:] = (whole - whole_hi.astype(f32)).astype(jnp.bfloat16)

    lax.fori_loop(DEG // 2, DEG, step, 0)

    save = pltpu.make_async_copy(y.at[DEG], out_ref, out_sem)
    save.start()
    both = lax.dot_general(
        y[DEG].reshape(blocks * nz, cols),
        m_ref[...],
        (((0,), (0,)), ((), ())),
        preferred_element_type=f32,
    )
    share = (both[:, :norb] + both[:, norb:]) * c1
    wide = norb // 128
    tiles = (cols // 8) * wide
    per = tiles // n_xy
    for t in range(tiles):
        part[t // per, (t % per) * 8 : (t % per + 1) * 8, :] = share[
            (t // wide) * 8 : (t // wide + 1) * 8, (t % wide) * 128 : (t % wide + 1) * 128
        ]

    me_xy = xx * ny + yy
    me_zc = (zh * nzl + zl) * 2 + core

    def plane_target(i):
        g = lax.rem(me_xy + i, n_xy)
        gy = lax.rem(g, ny)
        return g, ((zl * ny + gy) * 2 + core, (g // ny) * nzh + zh)

    def line_target(i):
        g = lax.rem(me_zc + i, n_zc)
        gz = g // 2
        return g, ((lax.rem(gz, nzl) * ny + yy) * 2 + lax.rem(g, 2), xx * nzh + gz // nzl)

    def exchange(stage, count, target_of, source_of, dst, mine):
        def send(i, carry):
            g, target = target_of(i)
            pltpu.make_async_remote_copy(
                src_ref=source_of(g),
                dst_ref=dst.at[mine],
                send_sem=rsend.at[stage],
                recv_sem=rrecv.at[stage],
                device_id=target,
                device_id_type=MESH,
            ).start()
            return carry

        lax.fori_loop(1, count, send, 0)

    def arrived(stage, count, target_of, dst):
        pltpu.make_async_remote_copy(
            src_ref=dst.at[pl.ds(0, count - 1)],
            dst_ref=dst.at[pl.ds(0, count - 1)],
            send_sem=rsend.at[stage],
            recv_sem=rrecv.at[stage],
            device_id=target_of(1)[1],
            device_id_type=MESH,
        ).wait()

    exchange(0, n_xy, plane_target, lambda g: part.at[g], rs, me_xy)
    rs[me_xy] = part[me_xy]
    arrived(0, n_xy, plane_target, rs)
    own = jnp.sum(rs[...], axis=0)
    ar_src[...] = own
    exchange(1, n_zc, line_target, lambda g: ar_src, ar, me_zc)
    ar[me_zc] = own
    arrived(1, n_zc, line_target, ar)
    own = jnp.sum(ar[...], axis=0)
    ag_src[...] = own
    exchange(2, n_xy, plane_target, lambda g: ag_src, ag, me_xy)
    ag[me_xy] = own
    arrived(2, n_xy, plane_target, ag)
    for t in range(tiles):
        inter_ref[
            (t // wide) * 8 : (t // wide + 1) * 8, (t % wide) * 128 : (t % wide + 1) * 128
        ] = ag[t // per, (t % per) * 8 : (t % per + 1) * 8, :]

    for side, buf in enumerate((hxl, hxh, hyl, hyh)):

        @pl.when(sends[side])
        def _(side=side, buf=buf):
            pltpu.make_async_remote_copy(
                src_ref=buf,
                dst_ref=buf,
                send_sem=hsend.at[side],
                recv_sem=hrecv.at[0, side, 0],
                device_id=(lax.rem(node + 1, n_node), orb),
                device_id_type=MESH,
            ).wait_send()

    pltpu.make_async_remote_copy(
        src_ref=abuf.at[pl.ds(0, n_node - 1)],
        dst_ref=abuf.at[pl.ds(0, n_node - 1)],
        send_sem=asend,
        recv_sem=arecv,
        device_id=(lax.rem(node + 1, n_node), orb),
        device_id_type=MESH,
    ).wait_send()
    save.wait()


def on_device(panel, orbitals, potential, projectors, strengths, atom_domain, patch_start):
    wx, wy, nz, cols = panel.shape
    norb = orbitals.shape[3]
    n_node = lax.axis_size("node")
    n_orb = lax.axis_size("orb")
    nzl, ny, nx, nzh = factors(n_node, n_orb)
    n_xy, n_zc = nx * ny, nzh * nzl * 2
    atoms = projectors.shape[0]
    nodes_all = n_node * wx * n_orb * wy * nz
    atoms_all = atoms * n_node * n_orb
    c1 = 1.0 / math.sqrt(nodes_all)
    ratio = math.sqrt(nodes_all) / math.sqrt(atoms_all)
    rows = (cols // 8) * (norb // 128) // n_xy * 8
    bf16, f32 = jnp.bfloat16, jnp.float32
    vmem = pl.BlockSpec(memory_space=pltpu.VMEM)
    hbm = pl.BlockSpec(memory_space=pl.ANY)
    dma = pltpu.SemaphoreType.DMA
    return pl.pallas_call(
        functools.partial(kernel, (n_node, n_orb, nzl, ny, nx, nzh), (c1, ratio)),
        out_shape=(
            jax.ShapeDtypeStruct(panel.shape, bf16),
            jax.ShapeDtypeStruct((cols, norb), f32),
        ),
        in_specs=[hbm, hbm] + [vmem] * 5,
        out_specs=(hbm, vmem),
        scratch_shapes=[
            pltpu.VMEM((DEG + 1, wx, wy, nz, cols), bf16),
            pltpu.VMEM((DEG, wy, nz, cols), bf16),
            pltpu.VMEM((DEG, wy, nz, cols), bf16),
            pltpu.VMEM((DEG, wx, nz, cols), bf16),
            pltpu.VMEM((DEG, wx, nz, cols), bf16),
            pltpu.VMEM((wx, wy, nz, cols), f32),
            pltpu.VMEM((wx, wy, nz, norb), bf16),
            pltpu.VMEM((2 * n_node, wx * wy * nz), bf16),
            pltpu.VMEM((wx * wy * nz, 2 * norb), bf16),
            pltpu.VMEM((n_node, 8, 128), f32),
            pltpu.VMEM((n_node, 8, 128), f32),
            pltpu.VMEM((n_xy, rows, 128), f32),
            pltpu.VMEM((n_xy, rows, 128), f32),
            pltpu.VMEM((rows, 128), f32),
            pltpu.VMEM((n_zc, rows, 128), f32),
            pltpu.VMEM((rows, 128), f32),
            pltpu.VMEM((n_xy, rows, 128), f32),
            dma((2,)),
            dma,
            dma((4,)),
            dma((DEG, 4, CHUNKS)),
            dma,
            dma,
            dma((3,)),
            dma((3,)),
        ],
        compiler_params=pltpu.CompilerParams(
            collective_id=0, has_side_effects=True, vmem_limit_bytes=48 * 1024 * 1024
        ),
    )(
        panel,
        orbitals,
        potential.reshape(wx * wy, nz),
        projectors,
        strengths.reshape(1, atoms),
        atom_domain.reshape(1, atoms),
        patch_start.reshape(1, atoms),
    )


def solution(mesh):
    placed = (
        P("node", "orb", None, None),
        P("node", "orb", None, None),
        P("node", "orb", None),
        P(("node", "orb"), None),
        P(("node", "orb")),
        P(("node", "orb"), None),
        P(("node", "orb")),
    )
    return jax.shard_map(
        on_device,
        mesh=mesh,
        in_specs=placed,
        out_specs=(P("node", "orb", None, None), P()),
        check_vma=False,
    )
```

```python
import functools
import math

import jax
import jax.numpy as jnp
from jax import lax
from jax.experimental import pallas as pl
from jax.experimental.pallas import tpu as pltpu
from jax.sharding import PartitionSpec as P

DEG = 6
CHUNKS = 4
MESH = pl.DeviceIdType.MESH
SHIFT_POINT = 5.25
HALF_RANGE = 3.25


def factors(count_node, count_orb):
    if (count_node, count_orb) == (48, 16):
        return 3, 8, 4, 4
    ny = max(1, min(count_node // 2, 8))
    return count_node // (2 * ny), ny, max(1, count_orb // 4), min(count_orb, 4)


def kernel(
    dims,
    scales,
    panel_ref,
    orbit_ref,
    pot_hbm,
    proj_hbm,
    str_hbm,
    dom_hbm,
    start_hbm,
    out_ref,
    inter_ref,
    y,
    hxl,
    hxh,
    hyl,
    hyh,
    diag,
    orb_v,
    pot_ref,
    proj_ref,
    str_ref,
    dom_ref,
    start_ref,
    w_ref,
    m_ref,
    apack,
    amid,
    abuf,
    pieces,
    crecv,
    part,
    rs,
    ar_src,
    ar,
    ag_src,
    ag,
    load_sem,
    out_sem,
    hsend,
    hrecv,
    asend,
    arecv,
    rsend,
    rrecv,
):
    n_node, n_orb, nzl, ny, nx, nzh = dims
    c1, ratio = scales
    node = lax.axis_index("node")
    orb = lax.axis_index("orb")
    core = lax.rem(node, 2)
    yy = lax.rem(node // 2, ny)
    zl = node // (2 * ny)
    xx = orb // nzh
    zh = lax.rem(orb, nzh)
    n_xy = nx * ny
    n_z = nzh * nzl
    n_yc = 2 * ny
    me_yc = lax.rem(node, n_yc)
    wx, wy, nz, cols = panel_ref.shape
    ch = nz // CHUNKS

    load_panel = pltpu.make_async_copy(panel_ref, y.at[0], load_sem.at[0])
    load_panel.start()
    load_orbit = pltpu.make_async_copy(orbit_ref, orb_v, load_sem.at[1])
    loads = [
        pltpu.make_async_copy(src, dst, load_sem.at[2 + i])
        for i, (src, dst) in enumerate(
            (
                (dom_hbm, dom_ref),
                (start_hbm, start_ref),
                (str_hbm, str_ref),
                (proj_hbm, proj_ref),
                (pot_hbm, pot_ref),
            )
        )
    ]
    for load in loads:
        load.start()
    load_orbit.start()

    barrier = pltpu.get_barrier_semaphore()

    def greet(target_node, target_orb):
        pl.semaphore_signal(
            barrier, inc=1, device_id=(target_node, target_orb), device_id_type=MESH
        )

    def greet_yc(i, carry):
        greet(zl * n_yc + lax.rem(me_yc + i, n_yc), orb)
        return carry

    lax.fori_loop(1, n_yc, greet_yc, 0)

    def greet_x(i, carry):
        gx = lax.rem(xx + 1 + i // ny, nx)
        gy = lax.rem(i, ny)
        greet((zl * ny + gy) * 2 + core, gx * nzh + zh)
        return carry

    lax.fori_loop(0, (nx - 1) * ny, greet_x, 0)
    me_z = zh * nzl + zl

    def z_target(i):
        g = lax.rem(me_z + i, n_z)
        return g, ((lax.rem(g, nzl) * ny + yy) * 2 + core, xx * nzh + g // nzl)

    def greet_z(i, carry):
        greet(*z_target(i)[1])
        return carry

    lax.fori_loop(1, n_z, greet_z, 0)
    greeted = (n_yc - 1) + (nx - 1) * ny + (n_z - 1)
    up_cross = jnp.logical_and(zh == nzh - 1, orb < n_orb - 1)
    down_cross = jnp.logical_and(zh == 0, orb > 0)

    up_seam = jnp.logical_and(me_yc == n_yc - 1, node < n_node - 1)
    down_seam = jnp.logical_and(me_yc == 0, node > 0)
    for crosses, target in (
        (up_cross, (node, orb + 1)),
        (down_cross, (node, orb - 1)),
        (up_seam, (node + 1, orb)),
        (down_seam, (node - 1, orb)),
    ):

        @pl.when(crosses)
        def _(target=target):
            greet(*target)

        greeted = greeted + crosses.astype(jnp.int32)

    pl.semaphore_wait(barrier, greeted)

    def halo(side, k, c):
        zs = pl.ds(c * ch, ch)
        if side == 0:
            src, dst, target = y.at[k, wx - 1, :, zs], hxl.at[k, :, zs], (node + 1, orb)
        elif side == 1:
            src, dst, target = y.at[k, 0, :, zs], hxh.at[k, :, zs], (node - 1, orb)
        elif side == 2:
            src, dst, target = y.at[k, :, wy - 1, zs], hyl.at[k, :, zs], (node, orb + 1)
        else:
            src, dst, target = y.at[k, :, 0, zs], hyh.at[k, :, zs], (node, orb - 1)
        return pltpu.make_async_remote_copy(
            src_ref=src,
            dst_ref=dst,
            send_sem=hsend.at[side],
            recv_sem=hrecv.at[k, side, c],
            device_id=target,
            device_id_type=MESH,
        )

    sends = (node < n_node - 1, node > 0, orb < n_orb - 1, orb > 0)
    receives = (node > 0, node < n_node - 1, orb > 0, orb < n_orb - 1)

    def send_halo(k, c, which):
        for side in which:

            @pl.when(sends[side])
            def _(side=side):
                halo(side, k, c).start()

    def wait_halo(k, c):
        for side in (0, 1, 2, 3):

            @pl.when(receives[side])
            def _(side=side):
                halo(side, k, c).wait_recv()

    load_panel.wait()
    for c in range(CHUNKS):
        send_halo(0, c, (2, 3))
    for c in range(CHUNKS):
        send_halo(0, c, (0, 1))

    for side, buf in enumerate((hxl, hxh, hyl, hyh)):

        @pl.when(jnp.logical_not(receives[side]))
        def _(buf=buf):
            def clear(k, carry):
                buf[k] = jnp.zeros(buf.shape[1:], buf.dtype)
                return carry

            lax.fori_loop(0, DEG, clear, 0)

    atoms = proj_ref.shape[0]
    for load in loads:
        load.wait()
    f32 = jnp.float32
    a_sub = lax.broadcasted_iota(jnp.int32, (atoms, atoms), 0)
    a_lane = lax.broadcasted_iota(jnp.int32, (atoms, atoms), 1)
    eye = a_sub == a_lane

    def column(row):
        return jnp.sum(jnp.where(eye, jnp.broadcast_to(row, (atoms, atoms)), 0), axis=1, keepdims=True)

    dom_row = dom_ref[...]
    start_row = start_ref[...]
    dom_col = column(dom_row)
    start_col = column(start_row)
    str_col = column(str_ref[...].astype(f32))
    hi_col = start_col // 128
    lo_col = start_col - hi_col * 128
    same = jnp.logical_and(jnp.broadcast_to(dom_col, (atoms, atoms)) == dom_row, a_sub < a_lane)
    rank_row = jnp.sum(jnp.where(same, 1, 0), axis=0, keepdims=True)
    halves = []
    for half in range(2):
        piece = proj_ref[:, half * 128 : (half + 1) * 128].astype(f32)
        for bit in range(7):
            taken = ((lo_col // (1 << bit)) - 2 * (lo_col // (2 << bit))) == 1
            piece = jnp.where(taken, pltpu.roll(piece, 1 << bit, 1), piece)
        halves.append(piece)
    lane = lax.broadcasted_iota(jnp.int32, (atoms, 128), 1)
    meta = jnp.where(
        lane == 0,
        lo_col.astype(f32),
        jnp.where(lane == 1, hi_col.astype(f32), jnp.where(lane == 2, str_col, 0.0)),
    )
    rows = lax.broadcasted_iota(jnp.int32, (n_node * 8, atoms), 0)
    slot_dom = rows // 8
    slot_row = rows - slot_dom * 8
    named = slot_dom == dom_row
    packed = None
    for code, piece in ((2 * rank_row, halves[0]), (2 * rank_row + 1, halves[1]), (4 + rank_row, meta)):
        choose = jnp.where(jnp.logical_and(named, slot_row == code), 1.0, 0.0)
        term = jnp.dot(choose, piece, preferred_element_type=f32)
        packed = term if packed is None else packed + term
    apack[...] = packed.reshape(nzl, n_yc, 8, 128)

    def send_atoms(i, carry):
        other = lax.rem(me_yc + i, n_yc)
        pltpu.make_async_remote_copy(
            src_ref=apack.at[:, other],
            dst_ref=amid.at[:, me_yc],
            send_sem=asend.at[0],
            recv_sem=arecv.at[0],
            device_id=(zl * n_yc + other, orb),
            device_id_type=MESH,
        ).start()
        return carry

    lax.fori_loop(1, n_yc, send_atoms, 0)
    amid[:, me_yc] = apack[:, me_yc]

    first_moved = pltpu.make_async_remote_copy(
        src_ref=amid.at[:, pl.ds(0, n_yc - 1)],
        dst_ref=amid.at[:, pl.ds(0, n_yc - 1)],
        send_sem=asend.at[0],
        recv_sem=arecv.at[0],
        device_id=(node + 1 - 2 * core, orb),
        device_id_type=MESH,
    )
    if nzl > 1:
        second_moved = pltpu.make_async_remote_copy(
            src_ref=abuf.at[pl.ds(0, nzl - 1)],
            dst_ref=abuf.at[pl.ds(0, nzl - 1)],
            send_sem=asend.at[1],
            recv_sem=arecv.at[1],
            device_id=(node + 1 - 2 * core, orb),
            device_id_type=MESH,
        )

    for ix in range(wx):
        for iy in range(wy):
            row = pot_ref[ix * wy + iy : ix * wy + iy + 1, :]
            diag[ix, iy] = (jnp.broadcast_to(row, (nz, nz)).T - (SHIFT_POINT - 3.0)) * (1.0 / HALF_RANGE)

    z_out = lax.broadcasted_iota(jnp.int32, (nz, nz), 0)
    z_in = lax.broadcasted_iota(jnp.int32, (nz, nz), 1)
    beside = jnp.where(jnp.abs(z_out - z_in) == 1, 1.0, 0.0).astype(jnp.bfloat16)

    def step(k, carry):
        twice = jnp.where(k == 0, 1.0, 2.0).astype(f32)
        less = jnp.where(k == 0, 0.0, 1.0).astype(f32)
        before = lax.max(k - 1, 0)
        arm = twice * (0.5 / HALF_RANGE)
        for c in range(CHUNKS):
            zs = pl.ds(c * ch, ch)
            here = [[y[k, ix, iy, zs].astype(f32) for iy in range(wy)] for ix in range(wx)]
            base = []
            for ix in range(wx):
                line = []
                for iy in range(wy):
                    total = jnp.dot(
                        beside[c * ch : (c + 1) * ch], y[k, ix, iy], preferred_element_type=f32
                    )
                    total = total + here[1 - ix][iy]
                    if iy > 0:
                        total = total + here[ix][iy - 1]
                    if iy < wy - 1:
                        total = total + here[ix][iy + 1]
                    old = y[before, ix, iy, zs].astype(f32)
                    line.append(
                        (twice * diag[ix, iy, zs]) * here[ix][iy] - arm * total - less * old
                    )
                base.append(line)
            wait_halo(k, c)
            for lines, which in (((0, wy - 1), (2, 3)), (range(1, wy - 1), (0, 1))):
                for iy in lines:
                    for ix in range(wx):
                        side = (hxl if ix == 0 else hxh)[k, iy, zs].astype(f32)
                        if iy == 0:
                            side = side + hyl[k, ix, zs].astype(f32)
                        if iy == wy - 1:
                            side = side + hyh[k, ix, zs].astype(f32)
                        y[k + 1, ix, iy, zs] = (base[ix][iy] - arm * side).astype(jnp.bfloat16)

                @pl.when(k < DEG - 1)
                def _(which=which, c=c):
                    send_halo(lax.min(k + 1, DEG - 1), c, which)

        return carry

    lax.fori_loop(0, 2, step, 0)

    first_moved.wait_recv()
    for ahead in range(1, nzl):
        other = lax.rem(zl + ahead, nzl)
        pltpu.make_async_remote_copy(
            src_ref=amid.at[other],
            dst_ref=abuf.at[zl],
            send_sem=asend.at[1],
            recv_sem=arecv.at[1],
            device_id=(other * n_yc + me_yc, orb),
            device_id_type=MESH,
        ).start()
    abuf[zl] = amid[zl]

    lax.fori_loop(2, 4, step, 0)

    if nzl > 1:
        second_moved.wait_recv()
    load_orbit.wait()
    blocks = wx * wy
    s_lane = lax.broadcasted_iota(jnp.int32, (n_node, 128), 1).astype(f32)
    coeffs = []
    for slot in range(2):
        v0 = abuf[:, :, 2 * slot, :].reshape(n_node, 128)
        v1 = abuf[:, :, 2 * slot + 1, :].reshape(n_node, 128)
        info = abuf[:, :, 4 + slot, :].reshape(n_node, 128)
        lo, hi, coeff = info[:, 0:1], info[:, 1:2], info[:, 2:3]
        inside = s_lane >= lo
        placed = (
            jnp.where(inside, v0, 0.0),
            jnp.where(inside, v1, v0),
            jnp.where(inside, 0.0, v1),
        )
        for j in range(blocks):
            total = jnp.zeros((n_node, 128), f32)
            for ahead in range(3):
                if j >= ahead:
                    total = total + jnp.where(hi == float(j - ahead), placed[ahead], 0.0)
            w_ref[slot * n_node : (slot + 1) * n_node, j * 128 : (j + 1) * 128] = total.astype(
                jnp.bfloat16
            )
        coeffs.append(coeff)
    flat_orbit = orb_v[...].reshape(blocks * nz, -1)
    norb = flat_orbit.shape[1]
    proj = jnp.dot(w_ref[...], flat_orbit, preferred_element_type=f32)
    proj = proj * (jnp.concatenate(coeffs, axis=0) * ratio)
    proj_hi = proj.astype(jnp.bfloat16)
    proj_lo = (proj - proj_hi.astype(f32)).astype(jnp.bfloat16)
    proj_both = jnp.concatenate([proj_hi, proj_lo], axis=1)
    for j in range(blocks):
        both = lax.dot_general(
            w_ref[:, j * 128 : (j + 1) * 128],
            proj_both,
            (((0,), (0,)), ((), ())),
            preferred_element_type=f32,
        )
        whole = both[:, :norb] + both[:, norb:] + orb_v[j // wy, j % wy].astype(f32)
        whole_hi = whole.astype(jnp.bfloat16)
        m_ref[j * 128 : (j + 1) * 128, :norb] = whole_hi
        m_ref[j * 128 : (j + 1) * 128, norb:] = (whole - whole_hi.astype(f32)).astype(jnp.bfloat16)

    lax.fori_loop(4, DEG, step, 0)

    save = pltpu.make_async_copy(y.at[DEG], out_ref, out_sem)
    save.start()
    both = lax.dot_general(
        y[DEG].reshape(blocks * nz, cols),
        m_ref[...],
        (((0,), (0,)), ((), ())),
        preferred_element_type=f32,
    )
    share = (both[:, :norb] + both[:, norb:]) * c1
    wide = norb // 128
    tiles = (cols // 8) * wide
    per = tiles // n_xy

    for t in range(tiles):
        for half in range(2):
            row = (t // wide) * 8 + half * 4
            pieces[half, t // per, (t % per) * 4 : (t % per + 1) * 4, :] = share[
                row : row + 4, (t % wide) * 128 : (t % wide + 1) * 128
            ]
    me_xy = xx * ny + yy
    across = (node + 1 - 2 * core, orb)

    def plane_target(i):
        g = lax.rem(me_xy + i, n_xy)
        return g, ((zl * ny + lax.rem(g, ny)) * 2 + core, (g // ny) * nzh + zh)

    def exchange(stage, count, target_of, source_of, dst, mine):
        def send(i, carry):
            g, target = target_of(i)
            pltpu.make_async_remote_copy(
                src_ref=source_of(g),
                dst_ref=dst.at[mine],
                send_sem=rsend.at[stage],
                recv_sem=rrecv.at[stage],
                device_id=target,
                device_id_type=MESH,
            ).start()
            return carry

        lax.fori_loop(1, count, send, 0)

    def moved(stage, ref):
        return pltpu.make_async_remote_copy(
            src_ref=ref,
            dst_ref=ref,
            send_sem=rsend.at[stage],
            recv_sem=rrecv.at[stage],
            device_id=across,
            device_id_type=MESH,
        )

    def to_core(stage, src, dst):
        return pltpu.make_async_remote_copy(
            src_ref=src,
            dst_ref=dst,
            send_sem=rsend.at[stage],
            recv_sem=rrecv.at[stage],
            device_id=across,
            device_id_type=MESH,
        )

    swap = to_core(0, pieces.at[1 - core], crecv)
    swap.start()
    swap.wait_recv()
    part[...] = pieces[core] + crecv[...]
    exchange(1, n_xy, plane_target, lambda g: part.at[g], rs, me_xy)
    rs[me_xy] = part[me_xy]
    moved(1, rs.at[pl.ds(0, n_xy - 1)]).wait_recv()
    own = jnp.sum(rs[...], axis=0)
    ar_src[...] = own
    exchange(2, n_z, z_target, lambda g: ar_src, ar, me_z)
    ar[me_z] = own
    moved(2, ar.at[pl.ds(0, n_z - 1)]).wait_recv()
    own = jnp.sum(ar[...], axis=0)
    ag_src[...] = own
    mine = ag.at[core]
    exchange(3, n_xy, plane_target, lambda g: ag_src, mine, me_xy)
    ag[core, me_xy] = own
    moved(3, mine.at[pl.ds(0, n_xy - 1)]).wait_recv()
    back = to_core(4, mine, mine)
    back.start()
    back.wait_recv()
    for t in range(tiles):
        for half in range(2):
            row = (t // wide) * 8 + half * 4
            inter_ref[row : row + 4, (t % wide) * 128 : (t % wide + 1) * 128] = ag[
                half, t // per, (t % per) * 4 : (t % per + 1) * 4, :
            ]

    for side, buf in enumerate((hxl, hxh, hyl, hyh)):

        @pl.when(sends[side])
        def _(side=side, buf=buf):
            pltpu.make_async_remote_copy(
                src_ref=buf,
                dst_ref=buf,
                send_sem=hsend.at[side],
                recv_sem=hrecv.at[0, side, 0],
                device_id=(lax.rem(node + 1, n_node), orb),
                device_id_type=MESH,
            ).wait_send()

    swap.wait_send()
    moved(1, rs.at[pl.ds(0, n_xy - 1)]).wait_send()
    moved(2, ar.at[pl.ds(0, n_z - 1)]).wait_send()
    moved(3, mine.at[pl.ds(0, n_xy - 1)]).wait_send()
    back.wait_send()
    first_moved.wait_send()
    if nzl > 1:
        second_moved.wait_send()
    save.wait()


def on_device(panel, orbitals, potential, projectors, strengths, atom_domain, patch_start):
    wx, wy, nz, cols = panel.shape
    norb = orbitals.shape[3]
    n_node = lax.axis_size("node")
    n_orb = lax.axis_size("orb")
    nzl, ny, nx, nzh = factors(n_node, n_orb)
    n_xy, n_z = nx * ny, nzh * nzl
    atoms = projectors.shape[0]
    nodes_all = n_node * wx * n_orb * wy * nz
    atoms_all = atoms * n_node * n_orb
    c1 = 1.0 / math.sqrt(nodes_all)
    ratio = math.sqrt(nodes_all) / math.sqrt(atoms_all)
    rows = (cols // 8) * (norb // 128) // n_xy * 4
    bf16, f32 = jnp.bfloat16, jnp.float32
    vmem = pl.BlockSpec(memory_space=pltpu.VMEM)
    hbm = pl.BlockSpec(memory_space=pltpu.HBM)
    dma = pltpu.SemaphoreType.DMA
    return pl.pallas_call(
        functools.partial(kernel, (n_node, n_orb, nzl, ny, nx, nzh), (c1, ratio)),
        out_shape=(
            jax.ShapeDtypeStruct(panel.shape, bf16),
            jax.ShapeDtypeStruct((cols, norb), f32),
        ),
        in_specs=[hbm] * 7,
        out_specs=(hbm, vmem),
        scratch_shapes=[
            pltpu.VMEM((DEG + 1, wx, wy, nz, cols), bf16),
            pltpu.VMEM((DEG, wy, nz, cols), bf16),
            pltpu.VMEM((DEG, wy, nz, cols), bf16),
            pltpu.VMEM((DEG, wx, nz, cols), bf16),
            pltpu.VMEM((DEG, wx, nz, cols), bf16),
            pltpu.VMEM((wx, wy, nz, cols), f32),
            pltpu.VMEM((wx, wy, nz, norb), bf16),
            pltpu.VMEM((wx * wy, nz), f32),
            pltpu.VMEM(projectors.shape, bf16),
            pltpu.VMEM((1, atoms), bf16),
            pltpu.VMEM((1, atoms), jnp.int32),
            pltpu.VMEM((1, atoms), jnp.int32),
            pltpu.VMEM((2 * n_node, wx * wy * nz), bf16),
            pltpu.VMEM((wx * wy * nz, 2 * norb), bf16),
            pltpu.VMEM((nzl, 2 * ny, 8, 128), f32),
            pltpu.VMEM((nzl, 2 * ny, 8, 128), f32),
            pltpu.VMEM((nzl, 2 * ny, 8, 128), f32),
            pltpu.VMEM((2, n_xy, rows, 128), f32),
            pltpu.VMEM((n_xy, rows, 128), f32),
            pltpu.VMEM((n_xy, rows, 128), f32),
            pltpu.VMEM((n_xy, rows, 128), f32),
            pltpu.VMEM((rows, 128), f32),
            pltpu.VMEM((n_z, rows, 128), f32),
            pltpu.VMEM((rows, 128), f32),
            pltpu.VMEM((2, n_xy, rows, 128), f32),
            dma((7,)),
            dma,
            dma((4,)),
            dma((DEG, 4, CHUNKS)),
            dma((2,)),
            dma((2,)),
            dma((5,)),
            dma((5,)),
        ],
        compiler_params=pltpu.CompilerParams(
            collective_id=0, has_side_effects=True, vmem_limit_bytes=63 * 1024 * 1024
        ),
    )(
        panel,
        orbitals,
        potential.reshape(wx * wy, nz),
        projectors,
        strengths.reshape(1, atoms),
        atom_domain.reshape(1, atoms),
        patch_start.reshape(1, atoms),
    )


def solution(mesh):
    placed = (
        P("node", "orb", None, None),
        P("node", "orb", None, None),
        P("node", "orb", None),
        P(("node", "orb"), None),
        P(("node", "orb")),
        P(("node", "orb"), None),
        P(("node", "orb")),
    )
    return jax.shard_map(
        on_device,
        mesh=mesh,
        in_specs=placed,
        out_specs=(P("node", "orb", None, None), P()),
        check_vma=False,
    )
```

```python
import functools
import math

import jax
import jax.numpy as jnp
from jax import lax
from jax.experimental import pallas as pl
from jax.experimental.pallas import tpu as pltpu
from jax.sharding import PartitionSpec as P

DEG = 6
CHUNKS = 4
MESH = pl.DeviceIdType.MESH
SHIFT_POINT = 5.25
HALF_RANGE = 3.25


def factors(count_node, count_orb):
    if (count_node, count_orb) == (48, 16):
        return 3, 8, 4, 4
    ny = max(1, min(count_node // 2, 8))
    return count_node // (2 * ny), ny, max(1, count_orb // 4), min(count_orb, 4)


def kernel(
    dims,
    scales,
    panel_ref,
    orbit_ref,
    pot_hbm,
    proj_hbm,
    str_hbm,
    dom_hbm,
    start_hbm,
    out_ref,
    inter_ref,
    y,
    hxl,
    hxh,
    hyl,
    hyh,
    diag,
    orb_v,
    pot_ref,
    proj_ref,
    str_ref,
    dom_ref,
    start_ref,
    w_ref,
    m_ref,
    apack,
    amid,
    abuf,
    pieces,
    part,
    rs,
    ar_src,
    ar,
    ag_src,
    ag,
    load_sem,
    out_sem,
    hsend,
    hrecv,
    asend,
    arecv,
    rsend,
    rrecv,
):
    n_node, n_orb, nzl, ny, nx, nzh = dims
    c1, ratio = scales
    node = lax.axis_index("node")
    orb = lax.axis_index("orb")
    core = lax.rem(node, 2)
    yy = lax.rem(node // 2, ny)
    zl = node // (2 * ny)
    xx = orb // nzh
    zh = lax.rem(orb, nzh)
    n_xy = nx * ny
    n_z = nzh * nzl
    n_yc = 2 * ny
    me_yc = lax.rem(node, n_yc)
    wx, wy, nz, cols = panel_ref.shape
    ch = nz // CHUNKS

    load_panel = pltpu.make_async_copy(panel_ref, y.at[0], load_sem.at[0])
    load_panel.start()
    load_orbit = pltpu.make_async_copy(orbit_ref, orb_v, load_sem.at[1])
    loads = [
        pltpu.make_async_copy(src, dst, load_sem.at[2 + i])
        for i, (src, dst) in enumerate(
            (
                (dom_hbm, dom_ref),
                (start_hbm, start_ref),
                (str_hbm, str_ref),
                (proj_hbm, proj_ref),
                (pot_hbm, pot_ref),
            )
        )
    ]
    for load in loads:
        load.start()
    load_orbit.start()

    barrier = pltpu.get_barrier_semaphore()

    def greet(target_node, target_orb):
        pl.semaphore_signal(
            barrier, inc=1, device_id=(target_node, target_orb), device_id_type=MESH
        )

    def greet_yc(i, carry):
        greet(zl * n_yc + lax.rem(me_yc + i, n_yc), orb)
        return carry

    lax.fori_loop(1, n_yc, greet_yc, 0)

    def greet_x(i, carry):
        gx = lax.rem(xx + 1 + i // ny, nx)
        gy = lax.rem(i, ny)
        greet((zl * ny + gy) * 2 + core, gx * nzh + zh)
        return carry

    lax.fori_loop(0, (nx - 1) * ny, greet_x, 0)
    me_z = zh * nzl + zl

    def z_target(i):
        g = lax.rem(me_z + i, n_z)
        return g, ((lax.rem(g, nzl) * ny + yy) * 2 + core, xx * nzh + g // nzl)

    def greet_z(i, carry):
        greet(*z_target(i)[1])
        return carry

    lax.fori_loop(1, n_z, greet_z, 0)
    greeted = (n_yc - 1) + (nx - 1) * ny + (n_z - 1)
    up_cross = jnp.logical_and(zh == nzh - 1, orb < n_orb - 1)
    down_cross = jnp.logical_and(zh == 0, orb > 0)

    up_seam = jnp.logical_and(me_yc == n_yc - 1, node < n_node - 1)
    down_seam = jnp.logical_and(me_yc == 0, node > 0)
    for crosses, target in (
        (up_cross, (node, orb + 1)),
        (down_cross, (node, orb - 1)),
        (up_seam, (node + 1, orb)),
        (down_seam, (node - 1, orb)),
    ):

        @pl.when(crosses)
        def _(target=target):
            greet(*target)

        greeted = greeted + crosses.astype(jnp.int32)

    pl.semaphore_wait(barrier, greeted)

    def halo(side, k, c):
        zs = pl.ds(c * ch, ch)
        if side == 0:
            src, dst, target = y.at[k, wx - 1, :, zs], hxl.at[k, :, zs], (node + 1, orb)
        elif side == 1:
            src, dst, target = y.at[k, 0, :, zs], hxh.at[k, :, zs], (node - 1, orb)
        elif side == 2:
            src, dst, target = y.at[k, :, wy - 1, zs], hyl.at[k, :, zs], (node, orb + 1)
        else:
            src, dst, target = y.at[k, :, 0, zs], hyh.at[k, :, zs], (node, orb - 1)
        return pltpu.make_async_remote_copy(
            src_ref=src,
            dst_ref=dst,
            send_sem=hsend.at[side],
            recv_sem=hrecv.at[k, side, c],
            device_id=target,
            device_id_type=MESH,
        )

    sends = (node < n_node - 1, node > 0, orb < n_orb - 1, orb > 0)
    receives = (node > 0, node < n_node - 1, orb > 0, orb < n_orb - 1)

    def send_halo(k, c, which):
        for side in which:

            @pl.when(sends[side])
            def _(side=side):
                halo(side, k, c).start()

    def wait_halo(k, c):
        for side in (0, 1, 2, 3):

            @pl.when(receives[side])
            def _(side=side):
                halo(side, k, c).wait_recv()

    load_panel.wait()
    for c in range(CHUNKS):
        send_halo(0, c, (2, 3))
    for c in range(CHUNKS):
        send_halo(0, c, (0, 1))

    for side, buf in enumerate((hxl, hxh, hyl, hyh)):

        @pl.when(jnp.logical_not(receives[side]))
        def _(buf=buf):
            def clear(k, carry):
                buf[k] = jnp.zeros(buf.shape[1:], buf.dtype)
                return carry

            lax.fori_loop(0, DEG, clear, 0)

    atoms = proj_ref.shape[0]
    for load in loads:
        load.wait()
    f32 = jnp.float32
    a_sub = lax.broadcasted_iota(jnp.int32, (atoms, atoms), 0)
    a_lane = lax.broadcasted_iota(jnp.int32, (atoms, atoms), 1)
    eye = a_sub == a_lane

    def column(row):
        return jnp.sum(jnp.where(eye, jnp.broadcast_to(row, (atoms, atoms)), 0), axis=1, keepdims=True)

    dom_row = dom_ref[...]
    start_row = start_ref[...]
    dom_col = column(dom_row)
    start_col = column(start_row)
    str_col = column(str_ref[...].astype(f32))
    hi_col = start_col // 128
    lo_col = start_col - hi_col * 128
    same = jnp.logical_and(jnp.broadcast_to(dom_col, (atoms, atoms)) == dom_row, a_sub < a_lane)
    rank_row = jnp.sum(jnp.where(same, 1, 0), axis=0, keepdims=True)
    halves = []
    for half in range(2):
        piece = proj_ref[:, half * 128 : (half + 1) * 128].astype(f32)
        for bit in range(7):
            taken = ((lo_col // (1 << bit)) - 2 * (lo_col // (2 << bit))) == 1
            piece = jnp.where(taken, pltpu.roll(piece, 1 << bit, 1), piece)
        halves.append(piece)
    lane = lax.broadcasted_iota(jnp.int32, (atoms, 128), 1)
    meta = jnp.where(
        lane == 0,
        lo_col.astype(f32),
        jnp.where(lane == 1, hi_col.astype(f32), jnp.where(lane == 2, str_col, 0.0)),
    )
    rows = lax.broadcasted_iota(jnp.int32, (n_node * 8, atoms), 0)
    slot_dom = rows // 8
    slot_row = rows - slot_dom * 8
    named = slot_dom == dom_row
    packed = None
    for code, piece in ((2 * rank_row, halves[0]), (2 * rank_row + 1, halves[1]), (4 + rank_row, meta)):
        choose = jnp.where(jnp.logical_and(named, slot_row == code), 1.0, 0.0)
        term = jnp.dot(choose, piece, preferred_element_type=f32)
        packed = term if packed is None else packed + term
    apack[...] = packed.reshape(nzl, n_yc, 8, 128)

    def send_atoms(i, carry):
        other = lax.rem(me_yc + i, n_yc)
        pltpu.make_async_remote_copy(
            src_ref=apack.at[:, other],
            dst_ref=amid.at[:, me_yc],
            send_sem=asend.at[0],
            recv_sem=arecv.at[0],
            device_id=(zl * n_yc + other, orb),
            device_id_type=MESH,
        ).start()
        return carry

    lax.fori_loop(1, n_yc, send_atoms, 0)
    amid[:, me_yc] = apack[:, me_yc]

    first_moved = pltpu.make_async_remote_copy(
        src_ref=amid.at[:, pl.ds(0, n_yc - 1)],
        dst_ref=amid.at[:, pl.ds(0, n_yc - 1)],
        send_sem=asend.at[0],
        recv_sem=arecv.at[0],
        device_id=(node + 1 - 2 * core, orb),
        device_id_type=MESH,
    )
    if nzl > 1:
        second_moved = pltpu.make_async_remote_copy(
            src_ref=abuf.at[pl.ds(0, nzl - 1)],
            dst_ref=abuf.at[pl.ds(0, nzl - 1)],
            send_sem=asend.at[1],
            recv_sem=arecv.at[1],
            device_id=(node + 1 - 2 * core, orb),
            device_id_type=MESH,
        )

    for ix in range(wx):
        for iy in range(wy):
            row = pot_ref[ix * wy + iy : ix * wy + iy + 1, :]
            diag[ix, iy] = (jnp.broadcast_to(row, (nz, nz)).T - (SHIFT_POINT - 3.0)) * (1.0 / HALF_RANGE)

    z_out = lax.broadcasted_iota(jnp.int32, (nz, nz), 0)
    z_in = lax.broadcasted_iota(jnp.int32, (nz, nz), 1)
    beside = jnp.where(jnp.abs(z_out - z_in) == 1, 1.0, 0.0).astype(jnp.bfloat16)

    def step(k, carry):
        twice = jnp.where(k == 0, 1.0, 2.0).astype(f32)
        less = jnp.where(k == 0, 0.0, 1.0).astype(f32)
        before = lax.max(k - 1, 0)
        arm = twice * (0.5 / HALF_RANGE)
        for c in range(CHUNKS):
            zs = pl.ds(c * ch, ch)
            here = [[y[k, ix, iy, zs].astype(f32) for iy in range(wy)] for ix in range(wx)]
            base = []
            for ix in range(wx):
                line = []
                for iy in range(wy):
                    total = jnp.dot(
                        beside[c * ch : (c + 1) * ch], y[k, ix, iy], preferred_element_type=f32
                    )
                    total = total + here[1 - ix][iy]
                    if iy > 0:
                        total = total + here[ix][iy - 1]
                    if iy < wy - 1:
                        total = total + here[ix][iy + 1]
                    old = y[before, ix, iy, zs].astype(f32)
                    line.append(
                        (twice * diag[ix, iy, zs]) * here[ix][iy] - arm * total - less * old
                    )
                base.append(line)
            wait_halo(k, c)
            for lines, which in (((0, wy - 1), (2, 3)), (range(1, wy - 1), (0, 1))):
                for iy in lines:
                    for ix in range(wx):
                        side = (hxl if ix == 0 else hxh)[k, iy, zs].astype(f32)
                        if iy == 0:
                            side = side + hyl[k, ix, zs].astype(f32)
                        if iy == wy - 1:
                            side = side + hyh[k, ix, zs].astype(f32)
                        y[k + 1, ix, iy, zs] = (base[ix][iy] - arm * side).astype(jnp.bfloat16)

                @pl.when(k < DEG - 1)
                def _(which=which, c=c):
                    send_halo(lax.min(k + 1, DEG - 1), c, which)

        return carry

    lax.fori_loop(0, 2, step, 0)

    first_moved.wait_recv()
    for ahead in range(1, nzl):
        other = lax.rem(zl + ahead, nzl)
        pltpu.make_async_remote_copy(
            src_ref=amid.at[other],
            dst_ref=abuf.at[zl],
            send_sem=asend.at[1],
            recv_sem=arecv.at[1],
            device_id=(other * n_yc + me_yc, orb),
            device_id_type=MESH,
        ).start()
    abuf[zl] = amid[zl]

    lax.fori_loop(2, 4, step, 0)

    if nzl > 1:
        second_moved.wait_recv()
    load_orbit.wait()
    blocks = wx * wy
    s_lane = lax.broadcasted_iota(jnp.int32, (n_node, 128), 1).astype(f32)
    coeffs = []
    for slot in range(2):
        v0 = abuf[:, :, 2 * slot, :].reshape(n_node, 128)
        v1 = abuf[:, :, 2 * slot + 1, :].reshape(n_node, 128)
        info = abuf[:, :, 4 + slot, :].reshape(n_node, 128)
        lo, hi, coeff = info[:, 0:1], info[:, 1:2], info[:, 2:3]
        inside = s_lane >= lo
        placed = (
            jnp.where(inside, v0, 0.0),
            jnp.where(inside, v1, v0),
            jnp.where(inside, 0.0, v1),
        )
        for j in range(blocks):
            total = jnp.zeros((n_node, 128), f32)
            for ahead in range(3):
                if j >= ahead:
                    total = total + jnp.where(hi == float(j - ahead), placed[ahead], 0.0)
            w_ref[slot * n_node : (slot + 1) * n_node, j * 128 : (j + 1) * 128] = total.astype(
                jnp.bfloat16
            )
        coeffs.append(coeff)
    flat_orbit = orb_v[...].reshape(blocks * nz, -1)
    norb = flat_orbit.shape[1]
    proj = jnp.dot(w_ref[...], flat_orbit, preferred_element_type=f32)
    proj = proj * (jnp.concatenate(coeffs, axis=0) * ratio)
    proj_hi = proj.astype(jnp.bfloat16)
    proj_lo = (proj - proj_hi.astype(f32)).astype(jnp.bfloat16)
    proj_both = jnp.concatenate([proj_hi, proj_lo], axis=1)
    for j in range(blocks):
        both = lax.dot_general(
            w_ref[:, j * 128 : (j + 1) * 128],
            proj_both,
            (((0,), (0,)), ((), ())),
            preferred_element_type=f32,
        )
        whole = both[:, :norb] + both[:, norb:] + orb_v[j // wy, j % wy].astype(f32)
        whole_hi = whole.astype(jnp.bfloat16)
        m_ref[j * 128 : (j + 1) * 128, :norb] = whole_hi
        m_ref[j * 128 : (j + 1) * 128, norb:] = (whole - whole_hi.astype(f32)).astype(jnp.bfloat16)

    lax.fori_loop(4, DEG, step, 0)

    save = pltpu.make_async_copy(y.at[DEG], out_ref, out_sem)
    save.start()
    both = lax.dot_general(
        y[DEG].reshape(blocks * nz, cols),
        m_ref[...],
        (((0,), (0,)), ((), ())),
        preferred_element_type=f32,
    )
    share = (both[:, :norb] + both[:, norb:]) * c1
    wide = norb // 128
    tiles = (cols // 8) * wide
    per = tiles // n_xy

    for t in range(tiles):
        part[t // per, (t % per) * 8 : (t % per + 1) * 8, :] = share[
            (t // wide) * 8 : (t // wide + 1) * 8, (t % wide) * 128 : (t % wide + 1) * 128
        ]
    me_xy = xx * ny + yy
    across = (node + 1 - 2 * core, orb)

    def plane_target(i):
        g = lax.rem(me_xy + i, n_xy)
        return g, ((zl * ny + lax.rem(g, ny)) * 2 + core, (g // ny) * nzh + zh)

    def exchange(stage, count, target_of, source_of, dst, mine):
        def send(i, carry):
            g, target = target_of(i)
            pltpu.make_async_remote_copy(
                src_ref=source_of(g),
                dst_ref=dst.at[mine],
                send_sem=rsend.at[stage],
                recv_sem=rrecv.at[stage],
                device_id=target,
                device_id_type=MESH,
            ).start()
            return carry

        lax.fori_loop(1, count, send, 0)

    def moved(stage, ref):
        return pltpu.make_async_remote_copy(
            src_ref=ref,
            dst_ref=ref,
            send_sem=rsend.at[stage],
            recv_sem=rrecv.at[stage],
            device_id=across,
            device_id_type=MESH,
        )

    def to_core(stage, src, dst):
        return pltpu.make_async_remote_copy(
            src_ref=src,
            dst_ref=dst,
            send_sem=rsend.at[stage],
            recv_sem=rrecv.at[stage],
            device_id=across,
            device_id_type=MESH,
        )

    exchange(1, n_xy, plane_target, lambda g: part.at[g], rs, me_xy)
    rs[me_xy] = part[me_xy]
    moved(1, rs.at[pl.ds(0, n_xy - 1)]).wait_recv()
    own = jnp.sum(rs[...], axis=0)
    pieces[core] = own
    swap = to_core(0, pieces.at[core], pieces.at[core])
    swap.start()
    swap.wait_recv()
    own = pieces[0] + pieces[1]
    ar_src[...] = own
    exchange(2, n_z, z_target, lambda g: ar_src, ar, me_z)
    ar[me_z] = own
    moved(2, ar.at[pl.ds(0, n_z - 1)]).wait_recv()
    own = jnp.sum(ar[...], axis=0)
    ag_src[...] = own
    exchange(3, n_xy, plane_target, lambda g: ag_src, ag, me_xy)
    ag[me_xy] = own
    moved(3, ag.at[pl.ds(0, n_xy - 1)]).wait_recv()
    for t in range(tiles):
        inter_ref[
            (t // wide) * 8 : (t // wide + 1) * 8, (t % wide) * 128 : (t % wide + 1) * 128
        ] = ag[t // per, (t % per) * 8 : (t % per + 1) * 8, :]

    for side, buf in enumerate((hxl, hxh, hyl, hyh)):

        @pl.when(sends[side])
        def _(side=side, buf=buf):
            pltpu.make_async_remote_copy(
                src_ref=buf,
                dst_ref=buf,
                send_sem=hsend.at[side],
                recv_sem=hrecv.at[0, side, 0],
                device_id=(lax.rem(node + 1, n_node), orb),
                device_id_type=MESH,
            ).wait_send()

    swap.wait_send()
    moved(1, rs.at[pl.ds(0, n_xy - 1)]).wait_send()
    moved(2, ar.at[pl.ds(0, n_z - 1)]).wait_send()
    moved(3, ag.at[pl.ds(0, n_xy - 1)]).wait_send()
    first_moved.wait_send()
    if nzl > 1:
        second_moved.wait_send()
    save.wait()


def on_device(panel, orbitals, potential, projectors, strengths, atom_domain, patch_start):
    wx, wy, nz, cols = panel.shape
    norb = orbitals.shape[3]
    n_node = lax.axis_size("node")
    n_orb = lax.axis_size("orb")
    nzl, ny, nx, nzh = factors(n_node, n_orb)
    n_xy, n_z = nx * ny, nzh * nzl
    atoms = projectors.shape[0]
    nodes_all = n_node * wx * n_orb * wy * nz
    atoms_all = atoms * n_node * n_orb
    c1 = 1.0 / math.sqrt(nodes_all)
    ratio = math.sqrt(nodes_all) / math.sqrt(atoms_all)
    rows = (cols // 8) * (norb // 128) // n_xy * 8
    bf16, f32 = jnp.bfloat16, jnp.float32
    vmem = pl.BlockSpec(memory_space=pltpu.VMEM)
    hbm = pl.BlockSpec(memory_space=pltpu.HBM)
    dma = pltpu.SemaphoreType.DMA
    return pl.pallas_call(
        functools.partial(kernel, (n_node, n_orb, nzl, ny, nx, nzh), (c1, ratio)),
        out_shape=(
            jax.ShapeDtypeStruct(panel.shape, bf16),
            jax.ShapeDtypeStruct((cols, norb), f32),
        ),
        in_specs=[hbm] * 7,
        out_specs=(hbm, vmem),
        scratch_shapes=[
            pltpu.VMEM((DEG + 1, wx, wy, nz, cols), bf16),
            pltpu.VMEM((DEG, wy, nz, cols), bf16),
            pltpu.VMEM((DEG, wy, nz, cols), bf16),
            pltpu.VMEM((DEG, wx, nz, cols), bf16),
            pltpu.VMEM((DEG, wx, nz, cols), bf16),
            pltpu.VMEM((wx, wy, nz, cols), f32),
            pltpu.VMEM((wx, wy, nz, norb), bf16),
            pltpu.VMEM((wx * wy, nz), f32),
            pltpu.VMEM(projectors.shape, bf16),
            pltpu.VMEM((1, atoms), bf16),
            pltpu.VMEM((1, atoms), jnp.int32),
            pltpu.VMEM((1, atoms), jnp.int32),
            pltpu.VMEM((2 * n_node, wx * wy * nz), bf16),
            pltpu.VMEM((wx * wy * nz, 2 * norb), bf16),
            pltpu.VMEM((nzl, 2 * ny, 8, 128), f32),
            pltpu.VMEM((nzl, 2 * ny, 8, 128), f32),
            pltpu.VMEM((nzl, 2 * ny, 8, 128), f32),
            pltpu.VMEM((2, rows, 128), f32),
            pltpu.VMEM((n_xy, rows, 128), f32),
            pltpu.VMEM((n_xy, rows, 128), f32),
            pltpu.VMEM((rows, 128), f32),
            pltpu.VMEM((n_z, rows, 128), f32),
            pltpu.VMEM((rows, 128), f32),
            pltpu.VMEM((n_xy, rows, 128), f32),
            dma((7,)),
            dma,
            dma((4,)),
            dma((DEG, 4, CHUNKS)),
            dma((2,)),
            dma((2,)),
            dma((5,)),
            dma((5,)),
        ],
        compiler_params=pltpu.CompilerParams(
            collective_id=0, has_side_effects=True, vmem_limit_bytes=63 * 1024 * 1024
        ),
    )(
        panel,
        orbitals,
        potential.reshape(wx * wy, nz),
        projectors,
        strengths.reshape(1, atoms),
        atom_domain.reshape(1, atoms),
        patch_start.reshape(1, atoms),
    )


def solution(mesh):
    placed = (
        P("node", "orb", None, None),
        P("node", "orb", None, None),
        P("node", "orb", None),
        P(("node", "orb"), None),
        P(("node", "orb")),
        P(("node", "orb"), None),
        P(("node", "orb")),
    )
    return jax.shard_map(
        on_device,
        mesh=mesh,
        in_specs=placed,
        out_specs=(P("node", "orb", None, None), P()),
        check_vma=False,
    )
```

```python
import functools
import math

import jax
import jax.numpy as jnp
from jax import lax
from jax.experimental import pallas as pl
from jax.experimental.pallas import tpu as pltpu
from jax.sharding import PartitionSpec as P

DEG = 6
CHUNKS = 4
MESH = pl.DeviceIdType.MESH
SHIFT_POINT = 5.25
HALF_RANGE = 3.25


def factors(count_node, count_orb):
    if (count_node, count_orb) == (48, 16):
        return 3, 8, 4, 4
    ny = max(1, min(count_node // 2, 8))
    return count_node // (2 * ny), ny, max(1, count_orb // 4), min(count_orb, 4)


def kernel(
    dims,
    scales,
    panel_ref,
    orbit_ref,
    pot_hbm,
    proj_hbm,
    str_hbm,
    dom_hbm,
    start_hbm,
    out_ref,
    inter_ref,
    y,
    hxl,
    hxh,
    hyl,
    hyh,
    diag,
    orb_v,
    pot_ref,
    proj_ref,
    str_ref,
    dom_ref,
    start_ref,
    w_ref,
    m_ref,
    apack,
    amid,
    abuf,
    pieces,
    part,
    rs,
    ar_src,
    ar,
    ag_src,
    ag,
    load_sem,
    out_sem,
    hsend,
    hrecv,
    asend,
    arecv,
    rsend,
    rrecv,
):
    n_node, n_orb, nzl, ny, nx, nzh = dims
    c1, ratio = scales
    node = lax.axis_index("node")
    orb = lax.axis_index("orb")
    core = lax.rem(node, 2)
    yy = lax.rem(node // 2, ny)
    zl = node // (2 * ny)
    xx = orb // nzh
    zh = lax.rem(orb, nzh)
    n_xy = nx * ny
    n_z = nzh * nzl
    n_yc = 2 * ny
    me_yc = lax.rem(node, n_yc)
    wx, wy, nz, cols = panel_ref.shape
    ch = nz // CHUNKS

    load_panel = pltpu.make_async_copy(panel_ref, y.at[0], load_sem.at[0])
    load_panel.start()
    load_orbit = pltpu.make_async_copy(orbit_ref, orb_v, load_sem.at[1])
    loads = [
        pltpu.make_async_copy(src, dst, load_sem.at[2 + i])
        for i, (src, dst) in enumerate(
            (
                (dom_hbm, dom_ref),
                (start_hbm, start_ref),
                (str_hbm, str_ref),
                (proj_hbm, proj_ref),
                (pot_hbm, pot_ref),
            )
        )
    ]
    for load in loads:
        load.start()
    load_orbit.start()

    barrier = pltpu.get_barrier_semaphore()

    def greet(target_node, target_orb):
        pl.semaphore_signal(
            barrier, inc=1, device_id=(target_node, target_orb), device_id_type=MESH
        )

    def greet_yc(i, carry):
        greet(zl * n_yc + lax.rem(me_yc + i, n_yc), orb)
        return carry

    lax.fori_loop(1, n_yc, greet_yc, 0)

    def greet_x(i, carry):
        gx = lax.rem(xx + 1 + i // ny, nx)
        gy = lax.rem(i, ny)
        greet((zl * ny + gy) * 2 + core, gx * nzh + zh)
        return carry

    lax.fori_loop(0, (nx - 1) * ny, greet_x, 0)
    me_z = zh * nzl + zl

    def z_target(i):
        step = i // 2
        step = jnp.where(lax.rem(i, 2) == 0, step, -step)
        g = lax.rem(me_z + n_z // 2 + step + n_z, n_z)
        return g, ((lax.rem(g, nzl) * ny + yy) * 2 + core, xx * nzh + g // nzl)

    def greet_z(i, carry):
        greet(*z_target(i)[1])
        return carry

    lax.fori_loop(1, n_z, greet_z, 0)
    greeted = (n_yc - 1) + (nx - 1) * ny + (n_z - 1)
    up_cross = jnp.logical_and(zh == nzh - 1, orb < n_orb - 1)
    down_cross = jnp.logical_and(zh == 0, orb > 0)

    up_seam = jnp.logical_and(me_yc == n_yc - 1, node < n_node - 1)
    down_seam = jnp.logical_and(me_yc == 0, node > 0)
    for crosses, target in (
        (up_cross, (node, orb + 1)),
        (down_cross, (node, orb - 1)),
        (up_seam, (node + 1, orb)),
        (down_seam, (node - 1, orb)),
    ):

        @pl.when(crosses)
        def _(target=target):
            greet(*target)

        greeted = greeted + crosses.astype(jnp.int32)

    pl.semaphore_wait(barrier, greeted)

    def halo(side, k, c):
        zs = pl.ds(c * ch, ch)
        if side == 0:
            src, dst, target = y.at[k, wx - 1, :, zs], hxl.at[k, :, zs], (node + 1, orb)
        elif side == 1:
            src, dst, target = y.at[k, 0, :, zs], hxh.at[k, :, zs], (node - 1, orb)
        elif side == 2:
            src, dst, target = y.at[k, :, wy - 1, zs], hyl.at[k, :, zs], (node, orb + 1)
        else:
            src, dst, target = y.at[k, :, 0, zs], hyh.at[k, :, zs], (node, orb - 1)
        return pltpu.make_async_remote_copy(
            src_ref=src,
            dst_ref=dst,
            send_sem=hsend.at[side],
            recv_sem=hrecv.at[k, side, c],
            device_id=target,
            device_id_type=MESH,
        )

    sends = (node < n_node - 1, node > 0, orb < n_orb - 1, orb > 0)
    receives = (node > 0, node < n_node - 1, orb > 0, orb < n_orb - 1)

    def send_halo(k, c, which):
        for side in which:

            @pl.when(sends[side])
            def _(side=side):
                halo(side, k, c).start()

    def wait_halo(k, c):
        for side in (0, 1, 2, 3):

            @pl.when(receives[side])
            def _(side=side):
                halo(side, k, c).wait_recv()

    load_panel.wait()
    for c in range(CHUNKS):
        send_halo(0, c, (2, 3, 0, 1))

    for side, buf in enumerate((hxl, hxh, hyl, hyh)):

        @pl.when(jnp.logical_not(receives[side]))
        def _(buf=buf):
            def clear(k, carry):
                buf[k] = jnp.zeros(buf.shape[1:], buf.dtype)
                return carry

            lax.fori_loop(0, DEG, clear, 0)

    atoms = proj_ref.shape[0]
    for load in loads:
        load.wait()
    f32 = jnp.float32
    a_sub = lax.broadcasted_iota(jnp.int32, (atoms, atoms), 0)
    a_lane = lax.broadcasted_iota(jnp.int32, (atoms, atoms), 1)
    eye = a_sub == a_lane

    def column(row):
        return jnp.sum(jnp.where(eye, jnp.broadcast_to(row, (atoms, atoms)), 0), axis=1, keepdims=True)

    dom_row = dom_ref[...]
    start_row = start_ref[...]
    dom_col = column(dom_row)
    start_col = column(start_row)
    str_col = column(str_ref[...].astype(f32))
    hi_col = start_col // 128
    lo_col = start_col - hi_col * 128
    same = jnp.logical_and(jnp.broadcast_to(dom_col, (atoms, atoms)) == dom_row, a_sub < a_lane)
    rank_row = jnp.sum(jnp.where(same, 1, 0), axis=0, keepdims=True)
    halves = []
    for half in range(2):
        piece = proj_ref[:, half * 128 : (half + 1) * 128].astype(f32)
        for bit in range(7):
            taken = ((lo_col // (1 << bit)) - 2 * (lo_col // (2 << bit))) == 1
            piece = jnp.where(taken, pltpu.roll(piece, 1 << bit, 1), piece)
        halves.append(piece)
    lane = lax.broadcasted_iota(jnp.int32, (atoms, 128), 1)
    meta = jnp.where(
        lane == 0,
        lo_col.astype(f32),
        jnp.where(lane == 1, hi_col.astype(f32), jnp.where(lane == 2, str_col, 0.0)),
    )
    rows = lax.broadcasted_iota(jnp.int32, (n_node * 8, atoms), 0)
    slot_dom = rows // 8
    slot_row = rows - slot_dom * 8
    named = slot_dom == dom_row
    packed = None
    for code, piece in ((2 * rank_row, halves[0]), (2 * rank_row + 1, halves[1]), (4 + rank_row, meta)):
        choose = jnp.where(jnp.logical_and(named, slot_row == code), 1.0, 0.0)
        term = jnp.dot(choose, piece, preferred_element_type=f32)
        packed = term if packed is None else packed + term
    apack[...] = packed.reshape(nzl, n_yc, 8, 128)

    def send_atoms(i, carry):
        other = lax.rem(me_yc + i, n_yc)
        pltpu.make_async_remote_copy(
            src_ref=apack.at[:, other],
            dst_ref=amid.at[:, me_yc],
            send_sem=asend.at[0],
            recv_sem=arecv.at[0],
            device_id=(zl * n_yc + other, orb),
            device_id_type=MESH,
        ).start()
        return carry

    lax.fori_loop(1, n_yc, send_atoms, 0)
    amid[:, me_yc] = apack[:, me_yc]

    first_moved = pltpu.make_async_remote_copy(
        src_ref=amid.at[:, pl.ds(0, n_yc - 1)],
        dst_ref=amid.at[:, pl.ds(0, n_yc - 1)],
        send_sem=asend.at[0],
        recv_sem=arecv.at[0],
        device_id=(node + 1 - 2 * core, orb),
        device_id_type=MESH,
    )
    if nzl > 1:
        second_moved = pltpu.make_async_remote_copy(
            src_ref=abuf.at[pl.ds(0, nzl - 1)],
            dst_ref=abuf.at[pl.ds(0, nzl - 1)],
            send_sem=asend.at[1],
            recv_sem=arecv.at[1],
            device_id=(node + 1 - 2 * core, orb),
            device_id_type=MESH,
        )

    for ix in range(wx):
        for iy in range(wy):
            row = pot_ref[ix * wy + iy : ix * wy + iy + 1, :]
            diag[ix, iy] = (jnp.broadcast_to(row, (nz, nz)).T - (SHIFT_POINT - 3.0)) * (1.0 / HALF_RANGE)

    z_out = lax.broadcasted_iota(jnp.int32, (nz, nz), 0)
    z_in = lax.broadcasted_iota(jnp.int32, (nz, nz), 1)
    beside = jnp.where(jnp.abs(z_out - z_in) == 1, 1.0, 0.0).astype(jnp.bfloat16)

    def step(k, carry):
        twice = jnp.where(k == 0, 1.0, 2.0).astype(f32)
        less = jnp.where(k == 0, 0.0, 1.0).astype(f32)
        before = lax.max(k - 1, 0)
        arm = twice * (0.5 / HALF_RANGE)
        for c in range(CHUNKS):
            zs = pl.ds(c * ch, ch)
            here = [[y[k, ix, iy, zs].astype(f32) for iy in range(wy)] for ix in range(wx)]
            base = []
            for ix in range(wx):
                line = []
                for iy in range(wy):
                    total = jnp.dot(
                        beside[c * ch : (c + 1) * ch], y[k, ix, iy], preferred_element_type=f32
                    )
                    total = total + here[1 - ix][iy]
                    if iy > 0:
                        total = total + here[ix][iy - 1]
                    if iy < wy - 1:
                        total = total + here[ix][iy + 1]
                    old = y[before, ix, iy, zs].astype(f32)
                    line.append(
                        (twice * diag[ix, iy, zs]) * here[ix][iy] - arm * total - less * old
                    )
                base.append(line)
            wait_halo(k, c)
            for lines, which in (((0, wy - 1), (2, 3)), (range(1, wy - 1), (0, 1))):
                for iy in lines:
                    for ix in range(wx):
                        side = (hxl if ix == 0 else hxh)[k, iy, zs].astype(f32)
                        if iy == 0:
                            side = side + hyl[k, ix, zs].astype(f32)
                        if iy == wy - 1:
                            side = side + hyh[k, ix, zs].astype(f32)
                        y[k + 1, ix, iy, zs] = (base[ix][iy] - arm * side).astype(jnp.bfloat16)

                @pl.when(k < DEG - 1)
                def _(which=which, c=c):
                    send_halo(lax.min(k + 1, DEG - 1), c, which)

        return carry

    lax.fori_loop(0, 2, step, 0)

    first_moved.wait_recv()
    for ahead in range(1, nzl):
        other = lax.rem(zl + ahead, nzl)
        pltpu.make_async_remote_copy(
            src_ref=amid.at[other],
            dst_ref=abuf.at[zl],
            send_sem=asend.at[1],
            recv_sem=arecv.at[1],
            device_id=(other * n_yc + me_yc, orb),
            device_id_type=MESH,
        ).start()
    abuf[zl] = amid[zl]

    lax.fori_loop(2, 4, step, 0)

    if nzl > 1:
        second_moved.wait_recv()
    load_orbit.wait()
    blocks = wx * wy
    s_lane = lax.broadcasted_iota(jnp.int32, (n_node, 128), 1).astype(f32)
    coeffs = []
    for slot in range(2):
        v0 = abuf[:, :, 2 * slot, :].reshape(n_node, 128)
        v1 = abuf[:, :, 2 * slot + 1, :].reshape(n_node, 128)
        info = abuf[:, :, 4 + slot, :].reshape(n_node, 128)
        lo, hi, coeff = info[:, 0:1], info[:, 1:2], info[:, 2:3]
        inside = s_lane >= lo
        placed = (
            jnp.where(inside, v0, 0.0),
            jnp.where(inside, v1, v0),
            jnp.where(inside, 0.0, v1),
        )
        for j in range(blocks):
            total = jnp.zeros((n_node, 128), f32)
            for ahead in range(3):
                if j >= ahead:
                    total = total + jnp.where(hi == float(j - ahead), placed[ahead], 0.0)
            w_ref[slot * n_node : (slot + 1) * n_node, j * 128 : (j + 1) * 128] = total.astype(
                jnp.bfloat16
            )
        coeffs.append(coeff)
    flat_orbit = orb_v[...].reshape(blocks * nz, -1)
    norb = flat_orbit.shape[1]
    proj = jnp.dot(w_ref[...], flat_orbit, preferred_element_type=f32)
    proj = proj * (jnp.concatenate(coeffs, axis=0) * ratio)
    proj_hi = proj.astype(jnp.bfloat16)
    proj_lo = (proj - proj_hi.astype(f32)).astype(jnp.bfloat16)
    proj_both = jnp.concatenate([proj_hi, proj_lo], axis=1)
    for j in range(blocks):
        both = lax.dot_general(
            w_ref[:, j * 128 : (j + 1) * 128],
            proj_both,
            (((0,), (0,)), ((), ())),
            preferred_element_type=f32,
        )
        whole = both[:, :norb] + both[:, norb:] + orb_v[j // wy, j % wy].astype(f32)
        whole_hi = whole.astype(jnp.bfloat16)
        m_ref[j * 128 : (j + 1) * 128, :norb] = whole_hi
        m_ref[j * 128 : (j + 1) * 128, norb:] = (whole - whole_hi.astype(f32)).astype(jnp.bfloat16)

    lax.fori_loop(4, DEG, step, 0)

    save = pltpu.make_async_copy(y.at[DEG], out_ref, out_sem)
    save.start()
    both = lax.dot_general(
        y[DEG].reshape(blocks * nz, cols),
        m_ref[...],
        (((0,), (0,)), ((), ())),
        preferred_element_type=f32,
    )
    share = (both[:, :norb] + both[:, norb:]) * c1
    wide = norb // 128
    tiles = (cols // 8) * wide
    per = tiles // n_xy

    for t in range(tiles):
        part[t // per, (t % per) * 8 : (t % per + 1) * 8, :] = share[
            (t // wide) * 8 : (t // wide + 1) * 8, (t % wide) * 128 : (t % wide + 1) * 128
        ]
    me_xy = xx * ny + yy
    across = (node + 1 - 2 * core, orb)

    def plane_target(i):
        i = i - 1
        dx, dy = i // ny, lax.rem(i, ny)
        dx = nx // 2 + jnp.where(lax.rem(dx, 2) == 0, dx // 2, -((dx + 1) // 2))
        dy = ny // 2 + jnp.where(lax.rem(dy, 2) == 0, dy // 2, -((dy + 1) // 2))
        g = lax.rem(xx + dx, nx) * ny + lax.rem(yy + dy, ny)
        return g, ((zl * ny + lax.rem(g, ny)) * 2 + core, (g // ny) * nzh + zh)

    def exchange(stage, count, target_of, source_of, dst, mine):
        def send(i, carry):
            g, target = target_of(i)
            pltpu.make_async_remote_copy(
                src_ref=source_of(g),
                dst_ref=dst.at[mine],
                send_sem=rsend.at[stage],
                recv_sem=rrecv.at[stage],
                device_id=target,
                device_id_type=MESH,
            ).start()
            return carry

        lax.fori_loop(1, count, send, 0)

    def moved(stage, ref):
        return pltpu.make_async_remote_copy(
            src_ref=ref,
            dst_ref=ref,
            send_sem=rsend.at[stage],
            recv_sem=rrecv.at[stage],
            device_id=across,
            device_id_type=MESH,
        )

    def to_core(stage, src, dst):
        return pltpu.make_async_remote_copy(
            src_ref=src,
            dst_ref=dst,
            send_sem=rsend.at[stage],
            recv_sem=rrecv.at[stage],
            device_id=across,
            device_id_type=MESH,
        )

    exchange(1, n_xy, plane_target, lambda g: part.at[g], rs, me_xy)
    rs[me_xy] = part[me_xy]
    moved(1, rs.at[pl.ds(0, n_xy - 1)]).wait_recv()
    own = jnp.sum(rs[...], axis=0)
    pieces[core] = own
    swap = to_core(0, pieces.at[core], pieces.at[core])
    swap.start()
    swap.wait_recv()
    own = pieces[0] + pieces[1]
    ar_src[...] = own
    exchange(2, n_z, z_target, lambda g: ar_src, ar, me_z)
    ar[me_z] = own
    moved(2, ar.at[pl.ds(0, n_z - 1)]).wait_recv()
    own = jnp.sum(ar[...], axis=0)
    ag_src[...] = own
    exchange(3, n_xy, plane_target, lambda g: ag_src, ag, me_xy)
    ag[me_xy] = own
    moved(3, ag.at[pl.ds(0, n_xy - 1)]).wait_recv()
    for t in range(tiles):
        inter_ref[
            (t // wide) * 8 : (t // wide + 1) * 8, (t % wide) * 128 : (t % wide + 1) * 128
        ] = ag[t // per, (t % per) * 8 : (t % per + 1) * 8, :]

    for side, buf in enumerate((hxl, hxh, hyl, hyh)):

        @pl.when(sends[side])
        def _(side=side, buf=buf):
            pltpu.make_async_remote_copy(
                src_ref=buf,
                dst_ref=buf,
                send_sem=hsend.at[side],
                recv_sem=hrecv.at[0, side, 0],
                device_id=(lax.rem(node + 1, n_node), orb),
                device_id_type=MESH,
            ).wait_send()

    swap.wait_send()
    moved(1, rs.at[pl.ds(0, n_xy - 1)]).wait_send()
    moved(2, ar.at[pl.ds(0, n_z - 1)]).wait_send()
    moved(3, ag.at[pl.ds(0, n_xy - 1)]).wait_send()
    first_moved.wait_send()
    if nzl > 1:
        second_moved.wait_send()
    save.wait()


def on_device(panel, orbitals, potential, projectors, strengths, atom_domain, patch_start):
    wx, wy, nz, cols = panel.shape
    norb = orbitals.shape[3]
    n_node = lax.axis_size("node")
    n_orb = lax.axis_size("orb")
    nzl, ny, nx, nzh = factors(n_node, n_orb)
    n_xy, n_z = nx * ny, nzh * nzl
    atoms = projectors.shape[0]
    nodes_all = n_node * wx * n_orb * wy * nz
    atoms_all = atoms * n_node * n_orb
    c1 = 1.0 / math.sqrt(nodes_all)
    ratio = math.sqrt(nodes_all) / math.sqrt(atoms_all)
    rows = (cols // 8) * (norb // 128) // n_xy * 8
    bf16, f32 = jnp.bfloat16, jnp.float32
    vmem = pl.BlockSpec(memory_space=pltpu.VMEM)
    hbm = pl.BlockSpec(memory_space=pltpu.HBM)
    dma = pltpu.SemaphoreType.DMA
    return pl.pallas_call(
        functools.partial(kernel, (n_node, n_orb, nzl, ny, nx, nzh), (c1, ratio)),
        out_shape=(
            jax.ShapeDtypeStruct(panel.shape, bf16),
            jax.ShapeDtypeStruct((cols, norb), f32),
        ),
        in_specs=[hbm] * 7,
        out_specs=(hbm, vmem),
        scratch_shapes=[
            pltpu.VMEM((DEG + 1, wx, wy, nz, cols), bf16),
            pltpu.VMEM((DEG, wy, nz, cols), bf16),
            pltpu.VMEM((DEG, wy, nz, cols), bf16),
            pltpu.VMEM((DEG, wx, nz, cols), bf16),
            pltpu.VMEM((DEG, wx, nz, cols), bf16),
            pltpu.VMEM((wx, wy, nz, cols), f32),
            pltpu.VMEM((wx, wy, nz, norb), bf16),
            pltpu.VMEM((wx * wy, nz), f32),
            pltpu.VMEM(projectors.shape, bf16),
            pltpu.VMEM((1, atoms), bf16),
            pltpu.VMEM((1, atoms), jnp.int32),
            pltpu.VMEM((1, atoms), jnp.int32),
            pltpu.VMEM((2 * n_node, wx * wy * nz), bf16),
            pltpu.VMEM((wx * wy * nz, 2 * norb), bf16),
            pltpu.VMEM((nzl, 2 * ny, 8, 128), f32),
            pltpu.VMEM((nzl, 2 * ny, 8, 128), f32),
            pltpu.VMEM((nzl, 2 * ny, 8, 128), f32),
            pltpu.VMEM((2, rows, 128), f32),
            pltpu.VMEM((n_xy, rows, 128), f32),
            pltpu.VMEM((n_xy, rows, 128), f32),
            pltpu.VMEM((rows, 128), f32),
            pltpu.VMEM((n_z, rows, 128), f32),
            pltpu.VMEM((rows, 128), f32),
            pltpu.VMEM((n_xy, rows, 128), f32),
            dma((7,)),
            dma,
            dma((4,)),
            dma((DEG, 4, CHUNKS)),
            dma((2,)),
            dma((2,)),
            dma((5,)),
            dma((5,)),
        ],
        compiler_params=pltpu.CompilerParams(
            collective_id=0, has_side_effects=True, vmem_limit_bytes=63 * 1024 * 1024
        ),
    )(
        panel,
        orbitals,
        potential.reshape(wx * wy, nz),
        projectors,
        strengths.reshape(1, atoms),
        atom_domain.reshape(1, atoms),
        patch_start.reshape(1, atoms),
    )


def solution(mesh):
    placed = (
        P("node", "orb", None, None),
        P("node", "orb", None, None),
        P("node", "orb", None),
        P(("node", "orb"), None),
        P(("node", "orb")),
        P(("node", "orb"), None),
        P(("node", "orb")),
    )
    return jax.shard_map(
        on_device,
        mesh=mesh,
        in_specs=placed,
        out_specs=(P("node", "orb", None, None), P()),
        check_vma=False,
    )
```

```python
import functools
import math

import jax
import jax.numpy as jnp
from jax import lax
from jax.experimental import pallas as pl
from jax.experimental.pallas import tpu as pltpu
from jax.sharding import PartitionSpec as P

DEG = 6
CHUNKS = 4
MESH = pl.DeviceIdType.MESH
SHIFT_POINT = 5.25
HALF_RANGE = 3.25


def factors(count_node, count_orb):
    if (count_node, count_orb) == (48, 16):
        return 3, 8, 4, 4
    ny = max(1, min(count_node // 2, 8))
    return count_node // (2 * ny), ny, max(1, count_orb // 4), min(count_orb, 4)


def kernel(
    dims,
    scales,
    panel_ref,
    orbit_ref,
    pot_hbm,
    proj_hbm,
    str_hbm,
    dom_hbm,
    start_hbm,
    out_ref,
    inter_ref,
    y,
    hxl,
    hxh,
    hyl,
    hyh,
    diag,
    orb_v,
    pot_ref,
    proj_ref,
    str_ref,
    dom_ref,
    start_ref,
    w_ref,
    m_ref,
    apack,
    amid,
    abuf,
    pieces,
    part,
    rs,
    ar_src,
    ar,
    ag_src,
    ag,
    load_sem,
    out_sem,
    hsend,
    hrecv,
    asend,
    arecv,
    rsend,
    rrecv,
):
    n_node, n_orb, nzl, ny, nx, nzh = dims
    c1, ratio = scales
    node = lax.axis_index("node")
    orb = lax.axis_index("orb")
    core = lax.rem(node, 2)
    yy = lax.rem(node // 2, ny)
    zl = node // (2 * ny)
    xx = orb // nzh
    zh = lax.rem(orb, nzh)
    n_xy = nx * ny
    n_z = nzh * nzl
    n_yc = 2 * ny
    me_yc = lax.rem(node, n_yc)
    wx, wy, nz, cols = panel_ref.shape
    ch = nz // CHUNKS

    load_panel = pltpu.make_async_copy(panel_ref, y.at[0], load_sem.at[0])
    load_panel.start()
    load_orbit = pltpu.make_async_copy(orbit_ref, orb_v, load_sem.at[1])
    loads = [
        pltpu.make_async_copy(src, dst, load_sem.at[2 + i])
        for i, (src, dst) in enumerate(
            (
                (dom_hbm, dom_ref),
                (start_hbm, start_ref),
                (str_hbm, str_ref),
                (proj_hbm, proj_ref),
                (pot_hbm, pot_ref),
            )
        )
    ]
    for load in loads:
        load.start()
    load_orbit.start()

    barrier = pltpu.get_barrier_semaphore()

    def greet(target_node, target_orb):
        pl.semaphore_signal(
            barrier, inc=1, device_id=(target_node, target_orb), device_id_type=MESH
        )

    def greet_yc(i, carry):
        greet(zl * n_yc + lax.rem(me_yc + i, n_yc), orb)
        return carry


    def greet_x(i, carry):
        gx = lax.rem(xx + 1 + i // ny, nx)
        gy = lax.rem(i, ny)
        greet((zl * ny + gy) * 2 + core, gx * nzh + zh)
        return carry

    me_z = zh * nzl + zl

    def z_target(i):
        step = i // 2
        step = jnp.where(lax.rem(i, 2) == 0, step, -step)
        g = lax.rem(me_z + n_z // 2 + step + n_z, n_z)
        return g, ((lax.rem(g, nzl) * ny + yy) * 2 + core, xx * nzh + g // nzl)

    def greet_z(i, carry):
        greet(*z_target(i)[1])
        return carry

    lax.fori_loop(1, n_z, greet_z, 0)
    lax.fori_loop(0, (nx - 1) * ny, greet_x, 0)
    lax.fori_loop(1, n_yc, greet_yc, 0)
    greeted = (n_yc - 1) + (nx - 1) * ny + (n_z - 1)
    up_cross = jnp.logical_and(zh == nzh - 1, orb < n_orb - 1)
    down_cross = jnp.logical_and(zh == 0, orb > 0)

    up_seam = jnp.logical_and(me_yc == n_yc - 1, node < n_node - 1)
    down_seam = jnp.logical_and(me_yc == 0, node > 0)
    for crosses, target in (
        (up_cross, (node, orb + 1)),
        (down_cross, (node, orb - 1)),
        (up_seam, (node + 1, orb)),
        (down_seam, (node - 1, orb)),
    ):

        @pl.when(crosses)
        def _(target=target):
            greet(*target)

        greeted = greeted + crosses.astype(jnp.int32)

    pl.semaphore_wait(barrier, greeted)

    def halo(side, k, c):
        zs = pl.ds(c * ch, ch)
        if side == 0:
            src, dst, target = y.at[k, wx - 1, :, zs], hxl.at[k, :, zs], (node + 1, orb)
        elif side == 1:
            src, dst, target = y.at[k, 0, :, zs], hxh.at[k, :, zs], (node - 1, orb)
        elif side == 2:
            src, dst, target = y.at[k, :, wy - 1, zs], hyl.at[k, :, zs], (node, orb + 1)
        else:
            src, dst, target = y.at[k, :, 0, zs], hyh.at[k, :, zs], (node, orb - 1)
        return pltpu.make_async_remote_copy(
            src_ref=src,
            dst_ref=dst,
            send_sem=hsend.at[side],
            recv_sem=hrecv.at[k, side, c],
            device_id=target,
            device_id_type=MESH,
        )

    sends = (node < n_node - 1, node > 0, orb < n_orb - 1, orb > 0)
    receives = (node > 0, node < n_node - 1, orb > 0, orb < n_orb - 1)

    def send_halo(k, c, which):
        for side in which:

            @pl.when(sends[side])
            def _(side=side):
                halo(side, k, c).start()

    def wait_halo(k, c):
        for side in (0, 1, 2, 3):

            @pl.when(receives[side])
            def _(side=side):
                halo(side, k, c).wait_recv()

    load_panel.wait()
    for c in range(CHUNKS):
        send_halo(0, c, (2, 3, 0, 1))

    for side, buf in enumerate((hxl, hxh, hyl, hyh)):

        @pl.when(jnp.logical_not(receives[side]))
        def _(buf=buf):
            def clear(k, carry):
                buf[k] = jnp.zeros(buf.shape[1:], buf.dtype)
                return carry

            lax.fori_loop(0, DEG, clear, 0)

    atoms = proj_ref.shape[0]
    for load in loads:
        load.wait()
    f32 = jnp.float32
    a_sub = lax.broadcasted_iota(jnp.int32, (atoms, atoms), 0)
    a_lane = lax.broadcasted_iota(jnp.int32, (atoms, atoms), 1)
    eye = a_sub == a_lane

    def column(row):
        return jnp.sum(jnp.where(eye, jnp.broadcast_to(row, (atoms, atoms)), 0), axis=1, keepdims=True)

    dom_row = dom_ref[...]
    start_row = start_ref[...]
    dom_col = column(dom_row)
    start_col = column(start_row)
    str_col = column(str_ref[...].astype(f32))
    hi_col = start_col // 128
    lo_col = start_col - hi_col * 128
    same = jnp.logical_and(jnp.broadcast_to(dom_col, (atoms, atoms)) == dom_row, a_sub < a_lane)
    rank_row = jnp.sum(jnp.where(same, 1, 0), axis=0, keepdims=True)
    halves = []
    for half in range(2):
        piece = proj_ref[:, half * 128 : (half + 1) * 128].astype(f32)
        for bit in range(7):
            taken = ((lo_col // (1 << bit)) - 2 * (lo_col // (2 << bit))) == 1
            piece = jnp.where(taken, pltpu.roll(piece, 1 << bit, 1), piece)
        halves.append(piece)
    lane = lax.broadcasted_iota(jnp.int32, (atoms, 128), 1)
    meta = jnp.where(
        lane == 0,
        lo_col.astype(f32),
        jnp.where(lane == 1, hi_col.astype(f32), jnp.where(lane == 2, str_col, 0.0)),
    )
    rows = lax.broadcasted_iota(jnp.int32, (n_node * 8, atoms), 0)
    slot_dom = rows // 8
    slot_row = rows - slot_dom * 8
    named = slot_dom == dom_row
    packed = None
    for code, piece in ((2 * rank_row, halves[0]), (2 * rank_row + 1, halves[1]), (4 + rank_row, meta)):
        choose = jnp.where(jnp.logical_and(named, slot_row == code), 1.0, 0.0)
        term = jnp.dot(choose, piece, preferred_element_type=f32)
        packed = term if packed is None else packed + term
    apack[...] = packed.reshape(nzl, n_yc, 8, 128)

    def send_atoms(i, carry):
        other = lax.rem(me_yc + i, n_yc)
        pltpu.make_async_remote_copy(
            src_ref=apack.at[:, other],
            dst_ref=amid.at[:, me_yc],
            send_sem=asend.at[0],
            recv_sem=arecv.at[0],
            device_id=(zl * n_yc + other, orb),
            device_id_type=MESH,
        ).start()
        return carry

    lax.fori_loop(1, n_yc, send_atoms, 0)
    amid[:, me_yc] = apack[:, me_yc]

    first_moved = pltpu.make_async_remote_copy(
        src_ref=amid.at[:, pl.ds(0, n_yc - 1)],
        dst_ref=amid.at[:, pl.ds(0, n_yc - 1)],
        send_sem=asend.at[0],
        recv_sem=arecv.at[0],
        device_id=(node + 1 - 2 * core, orb),
        device_id_type=MESH,
    )
    if nzl > 1:
        second_moved = pltpu.make_async_remote_copy(
            src_ref=abuf.at[pl.ds(0, nzl - 1)],
            dst_ref=abuf.at[pl.ds(0, nzl - 1)],
            send_sem=asend.at[1],
            recv_sem=arecv.at[1],
            device_id=(node + 1 - 2 * core, orb),
            device_id_type=MESH,
        )

    for ix in range(wx):
        for iy in range(wy):
            row = pot_ref[ix * wy + iy : ix * wy + iy + 1, :]
            diag[ix, iy] = (jnp.broadcast_to(row, (nz, nz)).T - (SHIFT_POINT - 3.0)) * (1.0 / HALF_RANGE)

    z_out = lax.broadcasted_iota(jnp.int32, (nz, nz), 0)
    z_in = lax.broadcasted_iota(jnp.int32, (nz, nz), 1)
    beside = jnp.where(jnp.abs(z_out - z_in) == 1, 1.0, 0.0).astype(jnp.bfloat16)

    def step(k, carry):
        twice = jnp.where(k == 0, 1.0, 2.0).astype(f32)
        less = jnp.where(k == 0, 0.0, 1.0).astype(f32)
        before = lax.max(k - 1, 0)
        arm = twice * (0.5 / HALF_RANGE)
        for c in range(CHUNKS):
            zs = pl.ds(c * ch, ch)
            here = [[y[k, ix, iy, zs].astype(f32) for iy in range(wy)] for ix in range(wx)]
            base = []
            for ix in range(wx):
                line = []
                for iy in range(wy):
                    total = jnp.dot(
                        beside[c * ch : (c + 1) * ch], y[k, ix, iy], preferred_element_type=f32
                    )
                    total = total + here[1 - ix][iy]
                    if iy > 0:
                        total = total + here[ix][iy - 1]
                    if iy < wy - 1:
                        total = total + here[ix][iy + 1]
                    old = y[before, ix, iy, zs].astype(f32)
                    line.append(
                        (twice * diag[ix, iy, zs]) * here[ix][iy] - arm * total - less * old
                    )
                base.append(line)
            wait_halo(k, c)
            for lines, which in (((0, wy - 1), (2, 3)), (range(1, wy - 1), (0, 1))):
                for iy in lines:
                    for ix in range(wx):
                        side = (hxl if ix == 0 else hxh)[k, iy, zs].astype(f32)
                        if iy == 0:
                            side = side + hyl[k, ix, zs].astype(f32)
                        if iy == wy - 1:
                            side = side + hyh[k, ix, zs].astype(f32)
                        y[k + 1, ix, iy, zs] = (base[ix][iy] - arm * side).astype(jnp.bfloat16)

                @pl.when(k < DEG - 1)
                def _(which=which, c=c):
                    send_halo(lax.min(k + 1, DEG - 1), c, which)

        return carry

    lax.fori_loop(0, 2, step, 0)

    first_moved.wait_recv()
    for ahead in range(1, nzl):
        other = lax.rem(zl + ahead, nzl)
        pltpu.make_async_remote_copy(
            src_ref=amid.at[other],
            dst_ref=abuf.at[zl],
            send_sem=asend.at[1],
            recv_sem=arecv.at[1],
            device_id=(other * n_yc + me_yc, orb),
            device_id_type=MESH,
        ).start()
    abuf[zl] = amid[zl]

    lax.fori_loop(2, 4, step, 0)

    if nzl > 1:
        second_moved.wait_recv()
    load_orbit.wait()
    blocks = wx * wy
    s_lane = lax.broadcasted_iota(jnp.int32, (n_node, 128), 1).astype(f32)
    coeffs = []
    for slot in range(2):
        v0 = abuf[:, :, 2 * slot, :].reshape(n_node, 128)
        v1 = abuf[:, :, 2 * slot + 1, :].reshape(n_node, 128)
        info = abuf[:, :, 4 + slot, :].reshape(n_node, 128)
        lo, hi, coeff = info[:, 0:1], info[:, 1:2], info[:, 2:3]
        inside = s_lane >= lo
        placed = (
            jnp.where(inside, v0, 0.0),
            jnp.where(inside, v1, v0),
            jnp.where(inside, 0.0, v1),
        )
        for j in range(blocks):
            total = jnp.zeros((n_node, 128), f32)
            for ahead in range(3):
                if j >= ahead:
                    total = total + jnp.where(hi == float(j - ahead), placed[ahead], 0.0)
            w_ref[slot * n_node : (slot + 1) * n_node, j * 128 : (j + 1) * 128] = total.astype(
                jnp.bfloat16
            )
        coeffs.append(coeff)
    flat_orbit = orb_v[...].reshape(blocks * nz, -1)
    norb = flat_orbit.shape[1]
    proj = jnp.dot(w_ref[...], flat_orbit, preferred_element_type=f32)
    proj = proj * (jnp.concatenate(coeffs, axis=0) * ratio)
    proj_hi = proj.astype(jnp.bfloat16)
    proj_lo = (proj - proj_hi.astype(f32)).astype(jnp.bfloat16)
    proj_both = jnp.concatenate([proj_hi, proj_lo], axis=1)
    for j in range(blocks):
        both = lax.dot_general(
            w_ref[:, j * 128 : (j + 1) * 128],
            proj_both,
            (((0,), (0,)), ((), ())),
            preferred_element_type=f32,
        )
        whole = both[:, :norb] + both[:, norb:] + orb_v[j // wy, j % wy].astype(f32)
        whole_hi = whole.astype(jnp.bfloat16)
        m_ref[j * 128 : (j + 1) * 128, :norb] = whole_hi
        m_ref[j * 128 : (j + 1) * 128, norb:] = (whole - whole_hi.astype(f32)).astype(jnp.bfloat16)

    lax.fori_loop(4, DEG, step, 0)

    save = pltpu.make_async_copy(y.at[DEG], out_ref, out_sem)
    save.start()
    both = lax.dot_general(
        y[DEG].reshape(blocks * nz, cols),
        m_ref[...],
        (((0,), (0,)), ((), ())),
        preferred_element_type=f32,
    )
    share = (both[:, :norb] + both[:, norb:]) * c1
    wide = norb // 128
    tiles = (cols // 8) * wide
    per = tiles // n_xy

    for t in range(tiles):
        part[t // per, (t % per) * 8 : (t % per + 1) * 8, :] = share[
            (t // wide) * 8 : (t // wide + 1) * 8, (t % wide) * 128 : (t % wide + 1) * 128
        ]
    me_xy = xx * ny + yy
    across = (node + 1 - 2 * core, orb)

    def plane_target(i):
        i = i - 1
        dx, dy = i // ny, lax.rem(i, ny)
        dx = nx // 2 + jnp.where(lax.rem(dx, 2) == 0, dx // 2, -((dx + 1) // 2))
        dy = ny // 2 + jnp.where(lax.rem(dy, 2) == 0, dy // 2, -((dy + 1) // 2))
        g = lax.rem(xx + dx, nx) * ny + lax.rem(yy + dy, ny)
        return g, ((zl * ny + lax.rem(g, ny)) * 2 + core, (g // ny) * nzh + zh)

    def exchange(stage, count, target_of, source_of, dst, mine):
        def send(i, carry):
            g, target = target_of(i)
            pltpu.make_async_remote_copy(
                src_ref=source_of(g),
                dst_ref=dst.at[mine],
                send_sem=rsend.at[stage],
                recv_sem=rrecv.at[stage],
                device_id=target,
                device_id_type=MESH,
            ).start()
            return carry

        lax.fori_loop(1, count, send, 0)

    def moved(stage, ref):
        return pltpu.make_async_remote_copy(
            src_ref=ref,
            dst_ref=ref,
            send_sem=rsend.at[stage],
            recv_sem=rrecv.at[stage],
            device_id=across,
            device_id_type=MESH,
        )

    def to_core(stage, src, dst):
        return pltpu.make_async_remote_copy(
            src_ref=src,
            dst_ref=dst,
            send_sem=rsend.at[stage],
            recv_sem=rrecv.at[stage],
            device_id=across,
            device_id_type=MESH,
        )

    exchange(1, n_xy, plane_target, lambda g: part.at[g], rs, me_xy)
    rs[me_xy] = part[me_xy]
    moved(1, rs.at[pl.ds(0, n_xy - 1)]).wait_recv()
    own = jnp.sum(rs[...], axis=0)
    pieces[core] = own
    swap = to_core(0, pieces.at[core], pieces.at[core])
    swap.start()
    swap.wait_recv()
    own = pieces[0] + pieces[1]
    ar_src[...] = own
    exchange(2, n_z, z_target, lambda g: ar_src, ar, me_z)
    ar[me_z] = own
    moved(2, ar.at[pl.ds(0, n_z - 1)]).wait_recv()
    own = jnp.sum(ar[...], axis=0)
    ag_src[...] = own
    exchange(3, n_xy, plane_target, lambda g: ag_src, ag, me_xy)
    ag[me_xy] = own
    moved(3, ag.at[pl.ds(0, n_xy - 1)]).wait_recv()
    for t in range(tiles):
        inter_ref[
            (t // wide) * 8 : (t // wide + 1) * 8, (t % wide) * 128 : (t % wide + 1) * 128
        ] = ag[t // per, (t % per) * 8 : (t % per + 1) * 8, :]

    for side, buf in enumerate((hxl, hxh, hyl, hyh)):

        @pl.when(sends[side])
        def _(side=side, buf=buf):
            pltpu.make_async_remote_copy(
                src_ref=buf,
                dst_ref=buf,
                send_sem=hsend.at[side],
                recv_sem=hrecv.at[0, side, 0],
                device_id=(lax.rem(node + 1, n_node), orb),
                device_id_type=MESH,
            ).wait_send()

    swap.wait_send()
    moved(1, rs.at[pl.ds(0, n_xy - 1)]).wait_send()
    moved(2, ar.at[pl.ds(0, n_z - 1)]).wait_send()
    moved(3, ag.at[pl.ds(0, n_xy - 1)]).wait_send()
    first_moved.wait_send()
    if nzl > 1:
        second_moved.wait_send()
    save.wait()


def on_device(panel, orbitals, potential, projectors, strengths, atom_domain, patch_start):
    wx, wy, nz, cols = panel.shape
    norb = orbitals.shape[3]
    n_node = lax.axis_size("node")
    n_orb = lax.axis_size("orb")
    nzl, ny, nx, nzh = factors(n_node, n_orb)
    n_xy, n_z = nx * ny, nzh * nzl
    atoms = projectors.shape[0]
    nodes_all = n_node * wx * n_orb * wy * nz
    atoms_all = atoms * n_node * n_orb
    c1 = 1.0 / math.sqrt(nodes_all)
    ratio = math.sqrt(nodes_all) / math.sqrt(atoms_all)
    rows = (cols // 8) * (norb // 128) // n_xy * 8
    bf16, f32 = jnp.bfloat16, jnp.float32
    vmem = pl.BlockSpec(memory_space=pltpu.VMEM)
    hbm = pl.BlockSpec(memory_space=pltpu.HBM)
    dma = pltpu.SemaphoreType.DMA
    return pl.pallas_call(
        functools.partial(kernel, (n_node, n_orb, nzl, ny, nx, nzh), (c1, ratio)),
        out_shape=(
            jax.ShapeDtypeStruct(panel.shape, bf16),
            jax.ShapeDtypeStruct((cols, norb), f32),
        ),
        in_specs=[hbm] * 7,
        out_specs=(hbm, vmem),
        scratch_shapes=[
            pltpu.VMEM((DEG + 1, wx, wy, nz, cols), bf16),
            pltpu.VMEM((DEG, wy, nz, cols), bf16),
            pltpu.VMEM((DEG, wy, nz, cols), bf16),
            pltpu.VMEM((DEG, wx, nz, cols), bf16),
            pltpu.VMEM((DEG, wx, nz, cols), bf16),
            pltpu.VMEM((wx, wy, nz, cols), f32),
            pltpu.VMEM((wx, wy, nz, norb), bf16),
            pltpu.VMEM((wx * wy, nz), f32),
            pltpu.VMEM(projectors.shape, bf16),
            pltpu.VMEM((1, atoms), bf16),
            pltpu.VMEM((1, atoms), jnp.int32),
            pltpu.VMEM((1, atoms), jnp.int32),
            pltpu.VMEM((2 * n_node, wx * wy * nz), bf16),
            pltpu.VMEM((wx * wy * nz, 2 * norb), bf16),
            pltpu.VMEM((nzl, 2 * ny, 8, 128), f32),
            pltpu.VMEM((nzl, 2 * ny, 8, 128), f32),
            pltpu.VMEM((nzl, 2 * ny, 8, 128), f32),
            pltpu.VMEM((2, rows, 128), f32),
            pltpu.VMEM((n_xy, rows, 128), f32),
            pltpu.VMEM((n_xy, rows, 128), f32),
            pltpu.VMEM((rows, 128), f32),
            pltpu.VMEM((n_z, rows, 128), f32),
            pltpu.VMEM((rows, 128), f32),
            pltpu.VMEM((n_xy, rows, 128), f32),
            dma((7,)),
            dma,
            dma((4,)),
            dma((DEG, 4, CHUNKS)),
            dma((2,)),
            dma((2,)),
            dma((5,)),
            dma((5,)),
        ],
        compiler_params=pltpu.CompilerParams(
            collective_id=0, has_side_effects=True, vmem_limit_bytes=63 * 1024 * 1024
        ),
    )(
        panel,
        orbitals,
        potential.reshape(wx * wy, nz),
        projectors,
        strengths.reshape(1, atoms),
        atom_domain.reshape(1, atoms),
        patch_start.reshape(1, atoms),
    )


def solution(mesh):
    placed = (
        P("node", "orb", None, None),
        P("node", "orb", None, None),
        P("node", "orb", None),
        P(("node", "orb"), None),
        P(("node", "orb")),
        P(("node", "orb"), None),
        P(("node", "orb")),
    )
    return jax.shard_map(
        on_device,
        mesh=mesh,
        in_specs=placed,
        out_specs=(P("node", "orb", None, None), P()),
        check_vma=False,
    )
```
